128 devices in a mesh: pb: 8 (over y_lo, x), row: 16 (over z, y_hi, core).
Axes of the slice: x: 4, y: 4 (y_hi: 2, y_lo: 2; y = y_hi * 2 + y_lo), z: 4, core: 2. Of those that a mesh axis runs over, the one named last changes fastest.
Arguments:
- probe_picture_embedding: bfloat16 [16384, 1280], P(('pb', 'row')), may hold values from -8 to 8, as said below
- query_caption_features: bfloat16 [16384, 1024], P(('pb', 'row')), may hold values from -8 to 8, as said below
- ref_image: bfloat16 [32768, 1280], P(('pb', 'row')), may hold values from -8 to 8, as said below
- ref_text: bfloat16 [32768, 1024], P(('pb', 'row')), may hold values from -8 to 8, as said below
- image_head: bfloat16 [1280, 768], replicated, may hold values from -0.15625 to 0.15625
- text_head: bfloat16 [1024, 768], replicated, may hold values from -0.1875 to 0.1875
Outputs:
- pointwise_dependence: float32 [16384], P(('pb', 'row'))
The draws below stay inside these ranges and needn't reach their ends.
Inputs may be any that keep to these rules, and one draw needn't show every extreme that they name: `probe_picture_embedding`: image features of pairs of one concept lie near a common centre; the caption follows the image's concept in most pairs. `query_caption_features`: text features of pairs of one concept lie near a common centre. `ref_image`: drawn by the same law as the query image features. `ref_text`: drawn by the same law as the query text features.
All inputs are finite; a program needn't handle non-finite values.
Results may differ from the reference program's by a relative error of at most 0.0003.
Values may be sent and summed in bfloat16 or wider, within the bound.
A program may use at most 128 MiB of HBM per device.

```python
import jax
import jax.numpy as jnp
from jax import lax

EI = 1280
ET = 1024
E = 768
CLUSTERS = 256
QUERIES = 16384
REFS = 32768


def concept_ids(key, salt, count):
    base = jax.random.fold_in(key, salt)
    first = jax.random.randint(jax.random.fold_in(base, 1), (count,), 0, CLUSTERS)
    other = jax.random.randint(jax.random.fold_in(base, 2), (count,), 0, CLUSTERS)
    coin = jax.random.randint(jax.random.fold_in(base, 3), (count,), 0, 10)
    second = jnp.where(coin < 7, first, other)
    return (first, second)


def features(key, own, centre_salt, ids, width):
    centres = jax.random.normal(jax.random.fold_in(key, centre_salt), (CLUSTERS, width), jnp.float32)
    local = jax.random.fold_in(key, own)
    noise = 0.7 * jax.random.normal(local, (ids.shape[0], width), jnp.float32)
    values = centres[ids] + noise
    return jnp.clip(values, -8.0, 8.0).astype(jnp.bfloat16)


def draw_probe_picture_embedding(key, part):
    first, second = concept_ids(key, 11, QUERIES)
    return features(key, 21, 101, first, EI)


def draw_query_caption_features(key, part):
    first, second = concept_ids(key, 11, QUERIES)
    return features(key, 22, 102, second, ET)


def draw_ref_image(key, part):
    first, second = concept_ids(key, 12, REFS)
    return features(key, 23, 101, first, EI)


def draw_ref_text(key, part):
    first, second = concept_ids(key, 12, REFS)
    return features(key, 24, 102, second, ET)


def bell_draw(rng, dims, spread, limit, dtype=jnp.bfloat16):
    return jnp.clip(spread * jax.random.normal(rng, dims, jnp.float32), -limit, limit).astype(dtype)


def setup_inputs(seed: int = 0) -> dict:
    splits = jax.random.split(jax.random.key(seed), 7)
    probe_picture_embedding = draw_probe_picture_embedding(jax.random.fold_in(splits[6], 71), 0)
    query_caption_features = draw_query_caption_features(jax.random.fold_in(splits[6], 71), 0)
    ref_image = draw_ref_image(jax.random.fold_in(splits[6], 71), 0)
    ref_text = draw_ref_text(jax.random.fold_in(splits[6], 71), 0)
    image_head = bell_draw(splits[4], (EI, E), EI ** -0.5, 0.15625)
    text_head = bell_draw(splits[5], (ET, E), ET ** -0.5, 0.1875)
    return {"probe_picture_embedding": probe_picture_embedding, "query_caption_features": query_caption_features, "ref_image": ref_image, "ref_text": ref_text, "image_head": image_head, "text_head": text_head}


epsilon = 1e-05
smoothing_divisor = 0.1

def unit(values):
    width = values.shape[-1]
    scale = lax.rsqrt(lax.optimization_barrier(jnp.mean(values * values, axis=-1, keepdims=True)) + epsilon)
    return values * scale * width ** (-0.5)

def embed(image, text, image_head, text_head):
    emb_image = unit(jnp.dot(image, image_head, preferred_element_type=jnp.float32)).astype(jnp.bfloat16)
    emb_text = unit(jnp.dot(text, text_head, preferred_element_type=jnp.float32)).astype(jnp.bfloat16)
    return jnp.concatenate([emb_image, emb_text], axis=1)

def block_sums(queries, reference_pairs):
    width = queries.shape[1] // 2
    visual_similarity_table = jnp.dot(queries[:, :width], reference_pairs[:, :width].T, preferred_element_type=jnp.float32)
    wording_similarity_table = jnp.dot(queries[:, width:], reference_pairs[:, width:].T, preferred_element_type=jnp.float32)
    visual_affinity_entries = jnp.exp((visual_similarity_table - 1.0) / smoothing_divisor)
    wording_affinity_entries = jnp.exp((wording_similarity_table - 1.0) / smoothing_divisor)
    return jnp.stack([lax.optimization_barrier(jnp.sum(visual_affinity_entries, axis=1)), lax.optimization_barrier(jnp.sum(wording_affinity_entries, axis=1)), lax.optimization_barrier(jnp.sum(visual_affinity_entries * wording_affinity_entries, axis=1))], axis=0)

def evaluate_sample_dependence(sums, count):
    return jnp.log(sums[2] / count) - jnp.log(sums[0] / count) - jnp.log(sums[1] / count)

def reference(probe_picture_embedding, query_caption_features, ref_image, ref_text, image_head, text_head):
    queries = embed(probe_picture_embedding, query_caption_features, image_head, text_head)
    reference_pairs = embed(ref_image, ref_text, image_head, text_head)
    total = queries.shape[0]
    block = 512 if total % 512 == 0 else total
    blocks = queries.reshape(total // block, block, queries.shape[1])
    sums = lax.map(lambda piece: block_sums(piece, reference_pairs), blocks)
    sums = jnp.transpose(sums, (1, 0, 2)).reshape(3, total)
    return evaluate_sample_dependence(sums, reference_pairs.shape[0])
```

```python
import functools

import jax
import jax.numpy as jnp
from jax import lax
from jax.experimental import pallas as pl
from jax.experimental.pallas import tpu as pltpu
from jax.sharding import PartitionSpec as P

MESH = pl.DeviceIdType.MESH
EPS = 1e-05
RATE = 10.0 * 1.4426950408889634
E = 768
ROWS_Q = 128
ROWS_R = 256
HALF = 64
N = 4
NT = (((1,), (1,)), ((), ()))

GROUPS = (
    (("A", 0, 0), ("B", 0, 0), ("A", 2, 0), ("B", 0, 2)),
    (("A", -1, 0), ("B", 0, -1), ("A", 1, 0), ("B", 0, 1)),
    (("A", 0, -1), ("B", -1, 0), ("A", 0, 1), ("B", 1, 0)),
    (("A", -1, -1), ("B", -1, -1), ("A", -1, 1), ("B", 1, -1)),
    (("A", 1, -1), ("B", -1, 1), ("A", 1, 1), ("B", 1, 1)),
    (("A", 2, -1), ("B", -1, 2), ("A", 2, 1), ("B", 1, 2)),
    (("A", 0, 2), ("B", 2, 0), ("A", -1, 2), ("B", 2, -1)),
    (("A", 1, 2), ("B", 2, 1), ("A", 2, 2), ("B", 2, 2)),
)
PLACE = {half: i for i, half in enumerate(h for g in GROUPS for h in g)}
SOURCES = tuple((dy, dz) for dy in (0, 1, -1, 2) for dz in (0, 1, -1, 2))
PLANE_DIRS = ((1, 0), (-1, 0), (0, 1), (0, -1))
DEPTH = 3


def wrap(d):
    return (d + 1) % N - 1


def plane_items(direction):
    sy, sz = direction
    if sy:
        h = 0 if sy > 0 else 1
        return (
            ("A", 0, 0, None),
            ("B", 0, 0, None),
            ("A", -sy, 0, h),
            ("B", 0, -1, None),
            ("B", 0, 1, None),
            ("B", -sy, 0, h),
            ("B", 0, 2, None),
            ("B", -sy, -1, h),
            ("B", -sy, 1, h),
            ("B", -sy, 2, h),
        )
    h = 0 if sz > 0 else 1
    return (
        ("B", 0, 0, None),
        ("A", 0, 0, None),
        ("B", 0, -sz, h),
        ("A", -1, 0, None),
        ("A", 1, 0, None),
        ("A", 0, -sz, h),
        ("A", 2, 0, None),
        ("A", -1, -sz, h),
        ("A", 1, -sz, h),
        ("A", 2, -sz, h),
    )


def query_rows(half, dy, dz, part):
    start = PLACE[(half, wrap(dy), wrap(dz))] * HALF
    if part is None:
        return start, HALF
    return start + part * (HALF // 2), HALF // 2


def device_at(x, y, z, c):
    return ((y % 2) * N + x, z * 4 + (y // 2) * 2 + c)


def unit(values):
    scale = lax.rsqrt(jnp.mean(values * values, axis=-1, keepdims=True) + EPS)
    return values * scale * E ** (-0.5)


def kernel(
    qi_hbm, qt_hbm, ri_hbm, rt_hbm, hi_hbm, ht_hbm, out_ref,
    xi, xt, hi, ht, queries, refs, acc, give, take,
    load_sem, plane_send, plane_recv, line_send, line_recv, pair_send, pair_recv, sum_send, sum_recv,
):
    pb, row = lax.axis_index("pb"), lax.axis_index("row")
    x, y = pb % N, (row // 2) % 2 * 2 + pb // N
    z, c = row // 4, row % 2

    def plane(dy, dz):
        return device_at(x, (y + dy + N) % N, (z + dz + N) % N, c)

    def line(dx):
        return device_at((x + dx + N) % N, y, z, c)

    pair = device_at(x, y, z, 1 - c)

    loads = []
    for i, (src, dst) in enumerate(
        (
            (qi_hbm, xi.at[pl.ds(0, ROWS_Q)]),
            (ri_hbm, xi.at[pl.ds(ROWS_Q, ROWS_R)]),
            (hi_hbm, hi),
            (qt_hbm, xt.at[pl.ds(0, ROWS_Q)]),
            (rt_hbm, xt.at[pl.ds(ROWS_Q, ROWS_R)]),
            (ht_hbm, ht),
        )
    ):
        copy = pltpu.make_async_copy(src, dst, load_sem.at[i])
        copy.start()
        loads.append(copy)

    barrier = pltpu.get_barrier_semaphore()
    greeted = [plane(dy, dz) for dy, dz in SOURCES[1:]] + [line(1), line(-1), pair]
    for device in greeted:
        pl.semaphore_signal(barrier, inc=1, device_id=device, device_id_type=MESH)

    acc[...] = jnp.zeros_like(acc)

    def project(features, head, columns):
        made = unit(jnp.dot(features[...], head[...], preferred_element_type=jnp.float32))
        made = made.astype(jnp.bfloat16)
        queries[0:ROWS_Q, columns] = made[:ROWS_Q]
        refs[0:ROWS_R, columns] = made[ROWS_Q:]

    for copy in loads[:3]:
        copy.wait()
    project(xi, hi, slice(0, E))
    for copy in loads[3:]:
        copy.wait()
    project(xt, ht, slice(E, 2 * E))

    pl.semaphore_wait(barrier, len(greeted))

    plane_copies = []
    for k, direction in enumerate(PLANE_DIRS):
        copies = []
        for i, (half, dy, dz, part) in enumerate(plane_items(direction)):
            start, rows = query_rows(half, dy, dz, part)
            there, _ = query_rows(half, dy - direction[0], dz - direction[1], part)
            copies.append(
                pltpu.make_async_remote_copy(
                    src_ref=queries.at[pl.ds(start, rows)],
                    dst_ref=queries.at[pl.ds(there, rows)],
                    send_sem=plane_send.at[k, i],
                    recv_sem=plane_recv.at[k, i],
                    device_id=plane(*direction),
                    device_id_type=MESH,
                )
            )
        plane_copies.append(copies)

    line_copies = []
    for k, dx in enumerate((1, -1)):
        copies = []
        for j in range(6):
            if j < 4:
                start = ((j + 2 * k) % 4) * HALF
            else:
                start = (2 + j - 4) * ROWS_R + k * HALF
            there = (2 + j) * ROWS_R + k * HALF
            copies.append(
                pltpu.make_async_remote_copy(
                    src_ref=refs.at[pl.ds(start, HALF)],
                    dst_ref=refs.at[pl.ds(there, HALF)],
                    send_sem=line_send.at[k, j],
                    recv_sem=line_recv.at[k, j],
                    device_id=line(dx),
                    device_id_type=MESH,
                )
            )
        line_copies.append(copies)
    pair_copies = []
    for j in range(7):
        start = (1 + j) * ROWS_R if j else 0
        there = start + 2 * HALF if j else ROWS_R
        rows = 2 * HALF if j else ROWS_R
        pair_copies.append(
            pltpu.make_async_remote_copy(
                src_ref=refs.at[pl.ds(start, rows)],
                dst_ref=refs.at[pl.ds(there, rows)],
                send_sem=pair_send.at[j],
                recv_sem=pair_recv.at[j],
                device_id=pair,
                device_id_type=MESH,
            )
        )

    def plane_start(i):
        for copies in plane_copies:
            copies[i].start()

    def plane_wait(i):
        for copies in plane_copies:
            copies[i].wait_recv()

    def line_start(j):
        for copies in line_copies:
            copies[j].start()

    def line_wait(j):
        for copies in line_copies:
            copies[j].wait_recv()

    def tile(q0, r0, rows):
        lanes = pl.ds(q0, ROWS_R)
        q = queries[lanes, :]
        r = refs[pl.ds(r0, rows), :]
        gi = lax.dot_general(r[:, :E], q[:, :E], NT, preferred_element_type=jnp.float32)
        gt = lax.dot_general(r[:, E:], q[:, E:], NT, preferred_element_type=jnp.float32)
        ki, kt = jnp.exp2(gi * RATE), jnp.exp2(gt * RATE)
        for k, values in enumerate((ki, kt, ki * kt)):
            acc[k, :, lanes] += jnp.sum(values.reshape(rows // 8, 8, ROWS_R), axis=0)

    def work(g0, groups, b0, blocks):
        rows = blocks * ROWS_R
        pieces = 1 if rows <= 1024 else 2
        rows //= pieces

        def body(i, carry):
            q0 = pl.multiple_of((g0 + i) * ROWS_R, ROWS_R)
            for piece in range(pieces):
                tile(q0, b0 * ROWS_R + piece * rows, rows)
            return carry

        if groups == 1:
            for piece in range(pieces):
                tile(g0 * ROWS_R, b0 * ROWS_R + piece * rows, rows)
        else:
            lax.fori_loop(0, groups, body, 0)

    early = lax.broadcasted_iota(jnp.int32, (1, ROWS_Q), 1) < HALF

    def owned(dy, dz):
        a, b = (PLACE[(h, dy, dz)] // 2 * ROWS_Q for h in "AB")
        rows = []
        for k in range(3):
            sums = acc[k, :, a : a + ROWS_Q]
            if a != b:
                sums = jnp.where(early, sums, acc[k, :, b : b + ROWS_Q])
            rows.append(jnp.sum(sums, axis=0, keepdims=True))
        return jnp.concatenate(rows + [rows[0]] * 5, axis=0)

    sum_copies = {}

    def hand_back(dy, dz):
        i = SOURCES.index((dy, dz)) - 1
        give[i] = owned(dy, dz)
        copy = pltpu.make_async_remote_copy(
            src_ref=give.at[i],
            dst_ref=take.at[i],
            send_sem=sum_send.at[i],
            recv_sem=sum_recv.at[i],
            device_id=plane(dy, dz),
            device_id_type=MESH,
        )
        copy.start()
        sum_copies[i] = copy

    started = 0

    def plane_upto(count):
        nonlocal started
        while started < min(count, 10):
            plane_start(started)
            started += 1

    plane_upto(2)
    line_start(0)
    line_start(1)
    pair_copies[0].start()

    plane_wait(0)
    plane_upto(1 + DEPTH)
    line_wait(0)
    line_start(2)
    pair_copies[1].start()
    pair_copies[0].wait_recv()
    work(1, 1, 0, 2)

    plane_wait(1)
    plane_upto(2 + DEPTH)
    line_wait(1)
    line_start(3)
    pair_copies[2].start()
    work(2, 1, 0, 2)
    pair_copies[1].wait_recv()
    pair_copies[2].wait_recv()
    work(1, 2, 2, 2)

    plane_wait(2)
    plane_upto(3 + DEPTH)
    work(0, 1, 0, 4)
    line_wait(2)
    line_start(4)
    pair_copies[3].start()

    plane_wait(3)
    plane_upto(4 + DEPTH)
    work(3, 1, 0, 4)
    line_wait(3)
    line_start(5)
    pair_copies[4].start()
    pair_copies[3].wait_recv()
    pair_copies[4].wait_recv()
    work(0, 4, 4, 2)

    plane_wait(4)
    plane_upto(5 + DEPTH)
    work(4, 1, 0, 6)

    plane_wait(5)
    plane_upto(6 + DEPTH)
    line_wait(4)
    pair_copies[5].start()
    pair_copies[5].wait_recv()
    work(0, 5, 6, 1)

    plane_wait(6)
    plane_upto(7 + DEPTH)
    line_wait(5)
    pair_copies[6].start()
    work(5, 1, 0, 7)
    pair_copies[6].wait_recv()
    work(0, 6, 7, 1)

    plane_wait(7)
    work(6, 1, 0, 8)
    late = ((1, 2), (2, 1), (2, 2))
    for source in SOURCES[1:]:
        if source not in late:
            hand_back(*source)

    plane_wait(8)
    plane_wait(9)
    work(7, 1, 0, 8)
    for source in late:
        hand_back(*source)

    total = owned(0, 0)
    for i in range(15):
        sum_copies[i].wait_recv()
        total = total + take[i]
    out_ref[...] = total

    for copies in plane_copies + line_copies:
        for copy in copies:
            copy.wait_send()
    for copy in pair_copies:
        copy.wait_send()
    for i in range(15):
        sum_copies[i].wait_send()


def local(query_image, query_text, ref_image, ref_text, image_head, text_head):
    count = ref_image.shape[0] * lax.axis_size("pb") * lax.axis_size("row")
    dma = pltpu.SemaphoreType.DMA
    sums = pl.pallas_call(
        kernel,
        out_shape=jax.ShapeDtypeStruct((8, ROWS_Q), jnp.float32),
        in_specs=[pl.BlockSpec(memory_space=pl.ANY)] * 6,
        out_specs=pl.BlockSpec(memory_space=pltpu.VMEM),
        scratch_shapes=[
            pltpu.VMEM((ROWS_Q + ROWS_R, query_image.shape[1]), jnp.bfloat16),
            pltpu.VMEM((ROWS_Q + ROWS_R, query_text.shape[1]), jnp.bfloat16),
            pltpu.VMEM(image_head.shape, jnp.bfloat16),
            pltpu.VMEM(text_head.shape, jnp.bfloat16),
            pltpu.VMEM((16 * ROWS_Q, 2 * E), jnp.bfloat16),
            pltpu.VMEM((8 * ROWS_R, 2 * E), jnp.bfloat16),
            pltpu.VMEM((3, 8, 16 * ROWS_Q), jnp.float32),
            pltpu.VMEM((15, 8, ROWS_Q), jnp.float32),
            pltpu.VMEM((15, 8, ROWS_Q), jnp.float32),
            dma((6,)),
            dma((4, 10)),
            dma((4, 10)),
            dma((2, 6)),
            dma((2, 6)),
            dma((7,)),
            dma((7,)),
            dma((15,)),
            dma((15,)),
        ],
        compiler_params=pltpu.CompilerParams(
            collective_id=0, has_side_effects=True, vmem_limit_bytes=60 * 2**20
        ),
    )(query_image, query_text, ref_image, ref_text, image_head, text_head)
    return jnp.log(sums[2]) - jnp.log(sums[0]) - jnp.log(sums[1]) + jnp.log(jnp.float32(count))


def solution(mesh):
    split = P(("pb", "row"), None)
    return jax.shard_map(
        local,
        mesh=mesh,
        in_specs=(split, split, split, split, P(), P()),
        out_specs=P(("pb", "row")),
        check_vma=False,
    )
```

```python
import functools

import jax
import jax.numpy as jnp
from jax import lax
from jax.experimental import pallas as pl
from jax.experimental.pallas import tpu as pltpu
from jax.sharding import PartitionSpec as P

MESH = pl.DeviceIdType.MESH
EPS = 1e-05
RATE = 10.0 * 1.4426950408889634
E = 768
ROWS_Q = 128
ROWS_R = 256
HALF = 64
N = 4
NT = (((1,), (1,)), ((), ()))

GROUPS = (
    (("A", 0, 0), ("B", 0, 0), ("A", 2, 0), ("B", 0, 2)),
    (("A", -1, 0), ("B", 0, -1), ("A", 1, 0), ("B", 0, 1)),
    (("A", 0, -1), ("B", -1, 0), ("A", 0, 1), ("B", 1, 0)),
    (("A", -1, -1), ("B", -1, -1), ("A", -1, 1), ("B", 1, -1)),
    (("A", 1, -1), ("B", -1, 1), ("A", 1, 1), ("B", 1, 1)),
    (("A", 2, -1), ("B", -1, 2), ("A", 2, 1), ("B", 1, 2)),
    (("A", 0, 2), ("B", 2, 0), ("A", -1, 2), ("B", 2, -1)),
    (("A", 1, 2), ("B", 2, 1), ("A", 2, 2), ("B", 2, 2)),
)
PLACE = {half: i for i, half in enumerate(h for g in GROUPS for h in g)}
SOURCES = tuple((dy, dz) for dy in (0, 1, -1, 2) for dz in (0, 1, -1, 2))
PLANE_DIRS = ((1, 0), (-1, 0), (0, 1), (0, -1))


def wrap(d):
    return (d + 1) % N - 1


BOTH, IMAGE, TEXT = slice(0, 2 * E), slice(0, E), slice(E, 2 * E)


def plane_items(direction):
    s = sum(direction)
    h = 0 if s > 0 else 1
    items = (
        ("A", 0, 0, None, IMAGE),
        ("A", 0, 0, None, TEXT),
        ("B", 0, 0, None, BOTH),
        ("A", -s, 0, h, BOTH),
        ("B", 0, -1, None, BOTH),
        ("B", 0, 1, None, BOTH),
        ("B", -s, 0, h, BOTH),
        ("B", 0, 2, None, BOTH),
        ("B", -s, -1, h, BOTH),
        ("B", -s, 1, h, IMAGE),
        ("B", -s, 2, h, IMAGE),
        ("B", -s, 1, h, TEXT),
        ("B", -s, 2, h, TEXT),
    )
    if direction[0]:
        return items
    return tuple(("AB"["BA".index(half)], dz, dy, part, columns) for half, dy, dz, part, columns in items)


UPTO = (3, 5, 6, 7, 8, 9, 10, 12, 13)


def query_rows(half, dy, dz, part):
    start = PLACE[(half, wrap(dy), wrap(dz))] * HALF
    if part is None:
        return start, HALF
    return start + part * (HALF // 2), HALF // 2


def device_at(x, y, z, c):
    return ((y % 2) * N + x, z * 4 + (y // 2) * 2 + c)


def unit(values):
    scale = lax.rsqrt(jnp.mean(values * values, axis=-1, keepdims=True) + EPS)
    return values * scale * E ** (-0.5)


def kernel(
    qi_hbm, qt_hbm, ri_hbm, rt_hbm, hi_hbm, ht_hbm, out_ref,
    qi, qt, ri, rt, hi, ht, queries, refs, acc, kept, give, take,
    load_sem, plane_send, plane_recv, line_send, line_recv, pair_send, pair_recv, sum_send, sum_recv,
):
    pb, row = lax.axis_index("pb"), lax.axis_index("row")
    x, y = pb % N, (row // 2) % 2 * 2 + pb // N
    z, c = row // 4, row % 2

    def plane(dy, dz):
        return device_at(x, (y + dy + N) % N, (z + dz + N) % N, c)

    def line(dx):
        return device_at((x + dx + N) % N, y, z, c)

    pair = device_at(x, y, z, 1 - c)

    loads = []
    for i, (src, dst) in enumerate(
        (
            (qi_hbm, qi),
            (hi_hbm, hi),
            (qt_hbm, qt),
            (ht_hbm, ht),
            (ri_hbm, ri),
            (rt_hbm, rt),
        )
    ):
        copy = pltpu.make_async_copy(src, dst, load_sem.at[i])
        copy.start()
        loads.append(copy)

    barrier = pltpu.get_barrier_semaphore()
    greeted = [plane(dy, dz) for dy, dz in PLANE_DIRS] + [line(1), line(-1), pair]
    for device in greeted:
        pl.semaphore_signal(barrier, inc=1, device_id=device, device_id_type=MESH)

    acc[...] = jnp.zeros_like(acc)

    def project(features, head, rows, columns, into):
        made = unit(jnp.dot(features[...], head[...], preferred_element_type=jnp.float32))
        into[0:rows, columns] = made.astype(jnp.bfloat16)

    plane_copies = []
    for k, direction in enumerate(PLANE_DIRS):
        copies = []
        for i, (half, dy, dz, part, columns) in enumerate(plane_items(direction)):
            start, rows = query_rows(half, dy, dz, part)
            there, _ = query_rows(half, dy - direction[0], dz - direction[1], part)
            copies.append(
                pltpu.make_async_remote_copy(
                    src_ref=queries.at[pl.ds(start, rows), columns],
                    dst_ref=queries.at[pl.ds(there, rows), columns],
                    send_sem=plane_send.at[k, i],
                    recv_sem=plane_recv.at[k, i],
                    device_id=plane(*direction),
                    device_id_type=MESH,
                )
            )
        plane_copies.append(copies)

    line_copies = []
    for k, dx in enumerate((1, -1)):
        copies = []
        for j in range(6):
            if j < 4:
                start = ((j + 2 * k) % 4) * HALF
            else:
                start = (2 + j - 4) * ROWS_R + k * HALF
            there = (2 + j) * ROWS_R + k * HALF
            copies.append(
                pltpu.make_async_remote_copy(
                    src_ref=refs.at[pl.ds(start, HALF)],
                    dst_ref=refs.at[pl.ds(there, HALF)],
                    send_sem=line_send.at[k, j],
                    recv_sem=line_recv.at[k, j],
                    device_id=line(dx),
                    device_id_type=MESH,
                )
            )
        line_copies.append(copies)
    pair_copies = []
    for j in range(7):
        start = (1 + j) * ROWS_R if j else 0
        there = start + 2 * HALF if j else ROWS_R
        rows = 2 * HALF if j else ROWS_R
        pair_copies.append(
            pltpu.make_async_remote_copy(
                src_ref=refs.at[pl.ds(start, rows)],
                dst_ref=refs.at[pl.ds(there, rows)],
                send_sem=pair_send.at[j],
                recv_sem=pair_recv.at[j],
                device_id=pair,
                device_id_type=MESH,
            )
        )

    def plane_start(i):
        for copies in plane_copies:
            copies[i].start()

    def plane_wait(i):
        for copies in plane_copies:
            copies[i].wait_recv()

    def line_start(j):
        for copies in line_copies:
            copies[j].start()

    def line_wait(j):
        for copies in line_copies:
            copies[j].wait_recv()

    def affinity(q0, lanes, r0, rows, columns):
        gram = lax.dot_general(
            refs[pl.ds(r0, rows), columns],
            queries[pl.ds(q0, lanes), columns],
            NT,
            preferred_element_type=jnp.float32,
        )
        return jnp.exp2(gram * RATE)

    def add(k, q0, lanes, values):
        acc[k, :, pl.ds(q0, lanes)] += jnp.sum(values.reshape(-1, 8, lanes), axis=0)

    def tile(q0, r0, rows):
        ki = affinity(q0, ROWS_R, r0, rows, IMAGE)
        kt = affinity(q0, ROWS_R, r0, rows, TEXT)
        for k, values in enumerate((ki, kt, ki * kt)):
            add(k, q0, ROWS_R, values)

    def work(g0, groups, b0, blocks):
        rows = blocks * ROWS_R
        pieces = 1 if rows <= 1024 else 2
        rows //= pieces
        for g in range(g0, g0 + groups):
            for piece in range(pieces):
                tile(g * ROWS_R, b0 * ROWS_R + piece * rows, rows)

    early = lax.broadcasted_iota(jnp.int32, (1, ROWS_Q), 1) < HALF

    def owned(dy, dz):
        a, b = (PLACE[(h, dy, dz)] // 2 * ROWS_Q for h in "AB")
        rows = []
        for k in range(3):
            sums = acc[k, :, a : a + ROWS_Q]
            if a != b:
                sums = jnp.where(early, sums, acc[k, :, b : b + ROWS_Q])
            rows.append(jnp.sum(sums, axis=0, keepdims=True))
        return jnp.concatenate(rows + [rows[0]] * 5, axis=0)

    sum_copies = [
        pltpu.make_async_remote_copy(
            src_ref=give.at[i],
            dst_ref=take.at[i],
            send_sem=sum_send.at[i],
            recv_sem=sum_recv.at[i],
            device_id=plane(dy, dz),
            device_id_type=MESH,
        )
        for i, (dy, dz) in enumerate(SOURCES[1:])
    ]

    def hand_back(sources):
        which = [SOURCES.index(source) - 1 for source in sources]
        for i, source in zip(which, sources):
            give[i] = owned(*source)
        for i in which:
            sum_copies[i].start()

    started = 0

    def plane_upto(count):
        nonlocal started
        for i in range(started, count):
            plane_start(i)
        started = max(started, count)

    def plane_next(i):
        plane_wait(i)
        if i < len(UPTO):
            plane_upto(UPTO[i])

    loads[0].wait()
    loads[1].wait()
    project(qi, hi, ROWS_Q, IMAGE, queries)
    pl.semaphore_wait(barrier, len(greeted))
    plane_upto(1)
    loads[2].wait()
    loads[3].wait()
    project(qt, ht, ROWS_Q, TEXT, queries)
    plane_upto(3)
    loads[4].wait()
    project(ri, hi, ROWS_R, IMAGE, refs)
    loads[5].wait()
    project(rt, ht, ROWS_R, TEXT, refs)
    line_start(0)
    line_start(1)
    pair_copies[0].start()

    plane_next(0)
    plane_next(1)
    line_wait(0)
    line_start(2)
    pair_copies[1].start()
    pair_copies[0].wait_recv()
    work(1, 1, 0, 2)

    plane_next(2)
    line_wait(1)
    line_start(3)
    pair_copies[2].start()
    work(2, 1, 0, 2)
    pair_copies[1].wait_recv()
    pair_copies[2].wait_recv()
    work(1, 2, 2, 2)

    plane_next(3)
    work(0, 1, 0, 4)
    line_wait(2)
    line_start(4)
    pair_copies[3].start()

    plane_next(4)
    work(3, 1, 0, 4)
    line_wait(3)
    line_start(5)
    pair_copies[4].start()
    pair_copies[3].wait_recv()
    pair_copies[4].wait_recv()
    work(0, 4, 4, 2)

    plane_next(5)
    work(4, 1, 0, 6)

    plane_next(6)
    line_wait(4)
    pair_copies[5].start()
    pair_copies[5].wait_recv()
    work(0, 5, 6, 1)

    plane_next(7)
    line_wait(5)
    pair_copies[6].start()
    work(5, 1, 0, 7)
    pair_copies[6].wait_recv()
    work(0, 6, 7, 1)

    plane_next(8)
    work(6, 1, 0, 8)
    late = ((1, 2), (2, 1), (2, 2))
    hand_back([source for source in SOURCES[1:] if source not in late])

    last = 7 * ROWS_R
    plane_next(9)
    plane_next(10)
    for piece in range(2):
        ki = affinity(last, ROWS_R, piece * 1024, 1024, IMAGE)
        kept[pl.ds(piece * 1024, 1024), :] = ki
        add(0, last, ROWS_R, ki)
    plane_next(11)
    plane_next(12)
    for piece in range(2):
        kt = affinity(last, ROWS_R, piece * 1024, 1024, TEXT)
        add(1, last, ROWS_R, kt)
        add(2, last, ROWS_R, kt * kept[pl.ds(piece * 1024, 1024), :])
    hand_back(late)

    total = owned(0, 0)
    for i in range(15):
        sum_copies[i].wait_recv()
        total = total + take[i]
    out_ref[...] = total

    for copies in plane_copies + line_copies:
        for copy in copies:
            copy.wait_send()
    for copy in pair_copies:
        copy.wait_send()
    for copy in sum_copies:
        copy.wait_send()


def local(query_image, query_text, ref_image, ref_text, image_head, text_head):
    count = ref_image.shape[0] * lax.axis_size("pb") * lax.axis_size("row")
    dma = pltpu.SemaphoreType.DMA
    sums = pl.pallas_call(
        kernel,
        out_shape=jax.ShapeDtypeStruct((8, ROWS_Q), jnp.float32),
        in_specs=[pl.BlockSpec(memory_space=pl.ANY)] * 6,
        out_specs=pl.BlockSpec(memory_space=pltpu.VMEM),
        scratch_shapes=[
            pltpu.VMEM(query_image.shape, jnp.bfloat16),
            pltpu.VMEM(query_text.shape, jnp.bfloat16),
            pltpu.VMEM(ref_image.shape, jnp.bfloat16),
            pltpu.VMEM(ref_text.shape, jnp.bfloat16),
            pltpu.VMEM(image_head.shape, jnp.bfloat16),
            pltpu.VMEM(text_head.shape, jnp.bfloat16),
            pltpu.VMEM((16 * ROWS_Q, 2 * E), jnp.bfloat16),
            pltpu.VMEM((8 * ROWS_R, 2 * E), jnp.bfloat16),
            pltpu.VMEM((3, 8, 16 * ROWS_Q), jnp.float32),
            pltpu.VMEM((8 * ROWS_R, ROWS_R), jnp.float32),
            pltpu.VMEM((15, 8, ROWS_Q), jnp.float32),
            pltpu.VMEM((15, 8, ROWS_Q), jnp.float32),
            dma((6,)),
            dma((4, 13)),
            dma((4, 13)),
            dma((2, 6)),
            dma((2, 6)),
            dma((7,)),
            dma((7,)),
            dma((15,)),
            dma((15,)),
        ],
        compiler_params=pltpu.CompilerParams(
            collective_id=0, has_side_effects=True, vmem_limit_bytes=60 * 2**20
        ),
    )(query_image, query_text, ref_image, ref_text, image_head, text_head)
    return jnp.log(sums[2]) - jnp.log(sums[0]) - jnp.log(sums[1]) + jnp.log(jnp.float32(count))


def solution(mesh):
    split = P(("pb", "row"), None)
    return jax.shard_map(
        local,
        mesh=mesh,
        in_specs=(split, split, split, split, P(), P()),
        out_specs=P(("pb", "row")),
        check_vma=False,
    )
```

```python
import functools

import jax
import jax.numpy as jnp
from jax import lax
from jax.experimental import pallas as pl
from jax.experimental.pallas import tpu as pltpu
from jax.sharding import PartitionSpec as P

MESH = pl.DeviceIdType.MESH
EPS = 1e-05
RATE = 10.0 * 1.4426950408889634
E = 768
ROWS_Q = 128
ROWS_R = 256
HALF = 64
N = 4
NT = (((1,), (1,)), ((), ()))

GROUPS = (
    (("A", 0, 0), ("B", 0, 0), ("A", 2, 0), ("B", 0, 2)),
    (("A", -1, 0), ("B", 0, -1), ("A", 1, 0), ("B", 0, 1)),
    (("A", 0, -1), ("B", -1, 0), ("A", 0, 1), ("B", 1, 0)),
    (("A", -1, -1), ("B", -1, -1), ("A", -1, 1), ("B", 1, -1)),
    (("A", 2, -1), ("B", -1, 2), ("A", 2, 1), ("B", 1, 2)),
    (("A", 1, -1), ("B", -1, 1), ("A", 1, 1), ("B", 1, 1)),
    (("A", 2, 2), ("B", 2, 2), ("A", -1, 2), ("B", 2, -1)),
    (("A", 1, 2), ("B", 2, 1), ("A", 0, 2), ("B", 2, 0)),
)
PLACE = {half: i for i, half in enumerate(h for g in GROUPS for h in g)}
SOURCES = tuple((dy, dz) for dy in (0, 1, -1, 2) for dz in (0, 1, -1, 2))
PLANE_DIRS = ((1, 0), (-1, 0), (0, 1), (0, -1))


def wrap(d):
    return (d + 1) % N - 1


IMAGE, TEXT = slice(0, E), slice(E, 2 * E)


def plane_items(direction):
    s = sum(direction)
    h = 0 if s > 0 else 1
    items = (
        ("A", 0, 0, None),
        ("B", 0, 0, None),
        ("A", -s, 0, h),
        ("B", 0, -1, None),
        ("B", 0, 2, None),
        ("B", 0, 1, None),
        ("B", -s, 2, h),
        ("B", -s, -1, h),
        ("B", -s, 1, h),
        ("B", -s, 0, h),
    )
    if direction[0]:
        return items
    return tuple(("AB"["BA".index(half)], dz, dy, part) for half, dy, dz, part in items)


UPTO = (4, 4, 6, 6, 8, 10)


def query_rows(half, dy, dz, part):
    start = PLACE[(half, wrap(dy), wrap(dz))] * HALF
    if part is None:
        return start, HALF
    return start + part * (HALF // 2), HALF // 2


def device_at(x, y, z, c):
    return ((y % 2) * N + x, z * 4 + (y // 2) * 2 + c)


def unit(values):
    scale = lax.rsqrt(jnp.mean(values * values, axis=-1, keepdims=True) + EPS)
    return values * scale * E ** (-0.5)


def kernel(
    qi_hbm, qt_hbm, ri_hbm, rt_hbm, hi_hbm, ht_hbm, out_ref,
    qi, qt, ri, rt, hi, ht, queries, refs, acc, give, take,
    load_sem, plane_send, plane_recv, line_send, line_recv, pair_send, pair_recv, sum_send, sum_recv,
):
    pb, row = lax.axis_index("pb"), lax.axis_index("row")
    x, y = pb % N, (row // 2) % 2 * 2 + pb // N
    z, c = row // 4, row % 2

    def plane(dy, dz):
        return device_at(x, (y + dy + N) % N, (z + dz + N) % N, c)

    def line(dx):
        return device_at((x + dx + N) % N, y, z, c)

    pair = device_at(x, y, z, 1 - c)

    loads = []
    for i, (src, dst) in enumerate(
        (
            (qi_hbm, qi),
            (hi_hbm, hi),
            (qt_hbm, qt),
            (ht_hbm, ht),
            (ri_hbm, ri),
            (rt_hbm, rt),
        )
    ):
        copy = pltpu.make_async_copy(src, dst, load_sem.at[i])
        copy.start()
        loads.append(copy)

    barrier = pltpu.get_barrier_semaphore()
    greeted = [plane(dy, dz) for dy, dz in PLANE_DIRS] + [line(1), line(-1), pair]
    for device in greeted:
        pl.semaphore_signal(barrier, inc=1, device_id=device, device_id_type=MESH)

    acc[...] = jnp.zeros_like(acc)

    def project(features, head, rows, columns, into):
        made = unit(jnp.dot(features[...], head[...], preferred_element_type=jnp.float32))
        into[0:rows, columns] = made.astype(jnp.bfloat16)

    plane_copies = []
    for k, direction in enumerate(PLANE_DIRS):
        copies = []
        for i, (half, dy, dz, part) in enumerate(plane_items(direction)):
            start, rows = query_rows(half, dy, dz, part)
            there, _ = query_rows(half, dy - direction[0], dz - direction[1], part)
            copies.append(
                pltpu.make_async_remote_copy(
                    src_ref=queries.at[pl.ds(start, rows)],
                    dst_ref=queries.at[pl.ds(there, rows)],
                    send_sem=plane_send.at[k, i],
                    recv_sem=plane_recv.at[k, i],
                    device_id=plane(*direction),
                    device_id_type=MESH,
                )
            )
        plane_copies.append(copies)

    line_copies = []
    for k, dx in enumerate((1, -1)):
        copies = []
        for j in range(6):
            if j < 4:
                start = ((j + 2 * k) % 4) * HALF
            else:
                start = (2 + j - 4) * ROWS_R + k * HALF
            there = (2 + j) * ROWS_R + k * HALF
            copies.append(
                pltpu.make_async_remote_copy(
                    src_ref=refs.at[pl.ds(start, HALF)],
                    dst_ref=refs.at[pl.ds(there, HALF)],
                    send_sem=line_send.at[k, j],
                    recv_sem=line_recv.at[k, j],
                    device_id=line(dx),
                    device_id_type=MESH,
                )
            )
        line_copies.append(copies)
    pair_copies = []
    for j in range(7):
        start = (1 + j) * ROWS_R if j else 0
        there = start + 2 * HALF if j else ROWS_R
        rows = 2 * HALF if j else ROWS_R
        pair_copies.append(
            pltpu.make_async_remote_copy(
                src_ref=refs.at[pl.ds(start, rows)],
                dst_ref=refs.at[pl.ds(there, rows)],
                send_sem=pair_send.at[j],
                recv_sem=pair_recv.at[j],
                device_id=pair,
                device_id_type=MESH,
            )
        )

    def plane_start(i):
        for copies in plane_copies:
            copies[i].start()

    def plane_wait(i):
        for copies in plane_copies:
            copies[i].wait_recv()

    def line_start(j):
        for copies in line_copies:
            copies[j].start()

    def line_wait(j):
        for copies in line_copies:
            copies[j].wait_recv()

    def affinity(q0, lanes, r0, rows, columns):
        gram = lax.dot_general(
            refs[pl.ds(r0, rows), columns],
            queries[pl.ds(q0, lanes), columns],
            NT,
            preferred_element_type=jnp.float32,
        )
        return jnp.exp2(gram * RATE)

    def add(k, q0, lanes, values):
        acc[k, :, pl.ds(q0, lanes)] += jnp.sum(values.reshape(-1, 8, lanes), axis=0)

    def tile(q0, lanes, r0, rows):
        ki = affinity(q0, lanes, r0, rows, IMAGE)
        kt = affinity(q0, lanes, r0, rows, TEXT)
        for k, values in enumerate((ki, kt, ki * kt)):
            add(k, q0, lanes, values)

    def work(q0, lanes, b0, blocks):
        rows = blocks * ROWS_R
        pieces = 1 if rows <= 1024 else 2
        for piece in range(pieces):
            tile(q0, lanes, b0 * ROWS_R + piece * (rows // pieces), rows // pieces)

    def work_groups(g0, groups, b0, blocks):
        for g in range(g0, g0 + groups):
            work(g * ROWS_R, ROWS_R, b0, blocks)

    early = lax.broadcasted_iota(jnp.int32, (1, ROWS_Q), 1) < HALF

    def owned(dy, dz):
        a, b = (PLACE[(h, dy, dz)] // 2 * ROWS_Q for h in "AB")
        rows = []
        for k in range(3):
            sums = acc[k, :, a : a + ROWS_Q]
            if a != b:
                sums = jnp.where(early, sums, acc[k, :, b : b + ROWS_Q])
            rows.append(jnp.sum(sums, axis=0, keepdims=True))
        return jnp.concatenate(rows + [rows[0]], axis=0)

    sum_copies = [
        pltpu.make_async_remote_copy(
            src_ref=give.at[i],
            dst_ref=take.at[i],
            send_sem=sum_send.at[i],
            recv_sem=sum_recv.at[i],
            device_id=plane(dy, dz),
            device_id_type=MESH,
        )
        for i, (dy, dz) in enumerate(SOURCES[1:])
    ]

    def hand_back(sources):
        which = [SOURCES.index(source) - 1 for source in sources]
        for i, source in zip(which, sources):
            give[i] = owned(*source)
        for i in which:
            sum_copies[i].start()

    started = 0

    def plane_upto(count):
        nonlocal started
        for i in range(started, count):
            plane_start(i)
        started = max(started, count)

    def plane_next(i):
        plane_wait(i)
        if i < len(UPTO):
            plane_upto(UPTO[i])

    loads[0].wait()
    loads[1].wait()
    project(qi, hi, ROWS_Q, IMAGE, queries)
    loads[2].wait()
    loads[3].wait()
    project(qt, ht, ROWS_Q, TEXT, queries)
    pl.semaphore_wait(barrier, len(greeted))
    plane_upto(2)
    loads[4].wait()
    project(ri, hi, ROWS_R, IMAGE, refs)
    loads[5].wait()
    project(rt, ht, ROWS_R, TEXT, refs)
    pair_copies[0].start()
    line_start(0)
    line_start(1)
    line_start(2)

    def line_next(j):
        line_wait(j)
        if j < 3:
            line_start(j + 3)
        pair_copies[j + 1].start()

    plane_next(0)
    pair_copies[0].wait_recv()
    work_groups(1, 1, 0, 2)
    line_next(0)

    plane_next(1)
    work_groups(2, 1, 0, 2)
    pair_copies[1].wait_recv()
    work_groups(1, 2, 2, 1)
    line_next(1)

    plane_next(2)
    pair_copies[2].wait_recv()
    work_groups(0, 1, 0, 4)
    work_groups(1, 2, 3, 1)
    line_next(2)

    plane_next(3)
    pair_copies[3].wait_recv()
    work_groups(3, 1, 0, 5)
    work_groups(0, 3, 4, 1)
    line_next(3)

    plane_next(4)
    pair_copies[4].wait_recv()
    work_groups(4, 1, 0, 6)
    work_groups(0, 4, 5, 1)
    line_next(4)

    plane_next(5)
    pair_copies[5].wait_recv()
    work_groups(5, 1, 0, 7)
    work_groups(0, 5, 6, 1)

    line_next(5)
    pair_copies[6].wait_recv()
    work_groups(0, 6, 7, 1)

    plane_next(6)
    plane_next(7)
    work_groups(6, 1, 0, 8)
    late = ((1, 2), (2, 1), (0, 2), (2, 0))
    hand_back([source for source in SOURCES[1:] if source not in late])

    plane_next(8)
    plane_next(9)
    work_groups(7, 1, 0, 8)
    hand_back(late)

    total = owned(0, 0)
    for i in range(15):
        sum_copies[i].wait_recv()
        total = total + take[i]
    out_ref[...] = total

    for copies in plane_copies + line_copies:
        for copy in copies:
            copy.wait_send()
    for copy in pair_copies:
        copy.wait_send()
    for copy in sum_copies:
        copy.wait_send()


def local(query_image, query_text, ref_image, ref_text, image_head, text_head):
    count = ref_image.shape[0] * lax.axis_size("pb") * lax.axis_size("row")
    dma = pltpu.SemaphoreType.DMA
    sums = pl.pallas_call(
        kernel,
        out_shape=pltpu.VMEM((4, ROWS_Q), jnp.float32),
        in_specs=[pl.BlockSpec(memory_space=pltpu.HBM)] * 6,
        out_specs=pl.BlockSpec(memory_space=pltpu.VMEM),
        scratch_shapes=[
            pltpu.VMEM(query_image.shape, jnp.bfloat16),
            pltpu.VMEM(query_text.shape, jnp.bfloat16),
            pltpu.VMEM(ref_image.shape, jnp.bfloat16),
            pltpu.VMEM(ref_text.shape, jnp.bfloat16),
            pltpu.VMEM(image_head.shape, jnp.bfloat16),
            pltpu.VMEM(text_head.shape, jnp.bfloat16),
            pltpu.VMEM((16 * ROWS_Q, 2 * E), jnp.bfloat16),
            pltpu.VMEM((8 * ROWS_R, 2 * E), jnp.bfloat16),
            pltpu.VMEM((3, 8, 16 * ROWS_Q), jnp.float32),
            pltpu.VMEM((15, 4, ROWS_Q), jnp.float32),
            pltpu.VMEM((15, 4, ROWS_Q), jnp.float32),
            dma((6,)),
            dma((4, 10)),
            dma((4, 10)),
            dma((2, 6)),
            dma((2, 6)),
            dma((7,)),
            dma((7,)),
            dma((15,)),
            dma((15,)),
        ],
        compiler_params=pltpu.CompilerParams(
            collective_id=0, has_side_effects=True, vmem_limit_bytes=63 * 2**20
        ),
    )(query_image, query_text, ref_image, ref_text, image_head, text_head)
    return jnp.log(sums[2]) - jnp.log(sums[0]) - jnp.log(sums[1]) + jnp.log(jnp.float32(count))


def solution(mesh):
    split = P(("pb", "row"), None)
    return jax.shard_map(
        local,
        mesh=mesh,
        in_specs=(split, split, split, split, P(), P()),
        out_specs=P(("pb", "row")),
        check_vma=False,
    )
```

```python
import functools

import jax
import jax.numpy as jnp
from jax import lax
from jax.experimental import pallas as pl
from jax.experimental.pallas import tpu as pltpu
from jax.sharding import PartitionSpec as P

MESH = pl.DeviceIdType.MESH
EPS = 1e-05
RATE = 10.0 * 1.4426950408889634
E = 768
ROWS_Q = 128
ROWS_R = 256
HALF = 64
N = 4
NT = (((1,), (1,)), ((), ()))

GROUPS = (
    (("A", 0, 0), ("B", 0, 0), ("A", 2, 0), ("B", 0, 2)),
    (("A", -1, 0), ("B", 0, -1), ("A", 1, 0), ("B", 0, 1)),
    (("A", 0, -1), ("B", -1, 0), ("A", 0, 1), ("B", 1, 0)),
    (("A", -1, -1), ("B", -1, -1), ("A", -1, 1), ("B", 1, -1)),
    (("A", 2, -1), ("B", -1, 2), ("A", 2, 1), ("B", 1, 2)),
    (("A", 1, -1), ("B", -1, 1), ("A", 1, 1), ("B", 1, 1)),
    (("A", 2, 2), ("B", 2, 2), ("A", -1, 2), ("B", 2, -1)),
    (("A", 1, 2), ("B", 2, 1), ("A", 0, 2), ("B", 2, 0)),
)
PLACE = {half: i for i, half in enumerate(h for g in GROUPS for h in g)}
SOURCES = tuple((dy, dz) for dy in (0, 1, -1, 2) for dz in (0, 1, -1, 2))
PLANE_DIRS = ((1, 0), (-1, 0), (0, 1), (0, -1))


def wrap(d):
    return (d + 1) % N - 1


IMAGE, TEXT = slice(0, E), slice(E, 2 * E)


def plane_items(direction):
    s = sum(direction)
    h = 0 if s > 0 else 1
    items = (
        ("A", 0, 0, None),
        ("B", 0, 0, None),
        ("A", -s, 0, h),
        ("B", 0, -1, None),
        ("B", 0, 2, None),
        ("B", 0, 1, None),
        ("B", -s, 2, h),
        ("B", -s, -1, h),
        ("B", -s, 1, h),
        ("B", -s, 0, h),
    )
    if direction[0]:
        return items
    return tuple(("AB"["BA".index(half)], dz, dy, part) for half, dy, dz, part in items)


UPTO = (4, 4, 6, 6, 8, 10)


def query_rows(half, dy, dz, part):
    start = PLACE[(half, wrap(dy), wrap(dz))] * HALF
    if part is None:
        return start, HALF
    return start + part * (HALF // 2), HALF // 2


def device_at(x, y, z, c):
    return ((y % 2) * N + x, z * 4 + (y // 2) * 2 + c)


def unit(values):
    scale = lax.rsqrt(jnp.mean(values * values, axis=-1, keepdims=True) + EPS)
    return values * scale * E ** (-0.5)


def kernel(
    qi_hbm, qt_hbm, ri_hbm, rt_hbm, hi_hbm, ht_hbm, out_ref,
    qi, qt, ri, rt, hi, ht, queries, refs, acc, give, take,
    load_sem, plane_send, plane_recv, line_send, line_recv, pair_send, pair_recv, sum_send, sum_recv,
):
    pb, row = lax.axis_index("pb"), lax.axis_index("row")
    x, y = pb % N, (row // 2) % 2 * 2 + pb // N
    z, c = row // 4, row % 2

    def plane(dy, dz):
        return device_at(x, (y + dy + N) % N, (z + dz + N) % N, c)

    def line(dx):
        return device_at((x + dx + N) % N, y, z, c)

    pair = device_at(x, y, z, 1 - c)

    loads = []
    for i, (src, dst) in enumerate(
        (
            (qi_hbm, qi),
            (hi_hbm, hi),
            (qt_hbm, qt),
            (ht_hbm, ht),
            (ri_hbm, ri),
            (rt_hbm, rt),
        )
    ):
        copy = pltpu.make_async_copy(src, dst, load_sem.at[i])
        copy.start()
        loads.append(copy)

    barrier = pltpu.get_barrier_semaphore()
    greeted = [plane(dy, dz) for dy, dz in PLANE_DIRS] + [line(1), line(-1), pair]
    for device in greeted:
        pl.semaphore_signal(barrier, inc=1, device_id=device, device_id_type=MESH)

    acc[...] = jnp.zeros_like(acc)

    def project(features, head, rows, columns, into):
        made = unit(jnp.dot(features[...], head[...], preferred_element_type=jnp.float32))
        into[0:rows, columns] = made.astype(jnp.bfloat16)

    plane_copies = []
    for k, direction in enumerate(PLANE_DIRS):
        copies = []
        for i, (half, dy, dz, part) in enumerate(plane_items(direction)):
            start, rows = query_rows(half, dy, dz, part)
            there, _ = query_rows(half, dy - direction[0], dz - direction[1], part)
            copies.append(
                pltpu.make_async_remote_copy(
                    src_ref=queries.at[pl.ds(start, rows)],
                    dst_ref=queries.at[pl.ds(there, rows)],
                    send_sem=plane_send.at[k, i],
                    recv_sem=plane_recv.at[k, i],
                    device_id=plane(*direction),
                    device_id_type=MESH,
                )
            )
        plane_copies.append(copies)

    line_copies = []
    for k, dx in enumerate((1, -1)):
        copies = []
        for j in range(6):
            if j < 4:
                start = ((j + 2 * k) % 4) * HALF
            else:
                start = (2 + j - 4) * ROWS_R + k * HALF
            there = (2 + j) * ROWS_R + k * HALF
            copies.append(
                pltpu.make_async_remote_copy(
                    src_ref=refs.at[pl.ds(start, HALF)],
                    dst_ref=refs.at[pl.ds(there, HALF)],
                    send_sem=line_send.at[k, j],
                    recv_sem=line_recv.at[k, j],
                    device_id=line(dx),
                    device_id_type=MESH,
                )
            )
        line_copies.append(copies)
    pair_copies = []
    for j in range(7):
        start = (1 + j) * ROWS_R if j else 0
        there = start + 2 * HALF if j else ROWS_R
        rows = 2 * HALF if j else ROWS_R
        pair_copies.append(
            pltpu.make_async_remote_copy(
                src_ref=refs.at[pl.ds(start, rows)],
                dst_ref=refs.at[pl.ds(there, rows)],
                send_sem=pair_send.at[j],
                recv_sem=pair_recv.at[j],
                device_id=pair,
                device_id_type=MESH,
            )
        )

    def plane_start(i):
        for copies in plane_copies:
            copies[i].start()

    def plane_wait(i):
        for copies in plane_copies:
            copies[i].wait_recv()

    def line_start(j):
        for copies in line_copies:
            copies[j].start()

    def line_wait(j):
        for copies in line_copies:
            copies[j].wait_recv()

    def affinity(q0, lanes, r0, rows, columns):
        gram = lax.dot_general(
            refs[pl.ds(r0, rows), columns],
            queries[pl.ds(q0, lanes), columns],
            NT,
            preferred_element_type=jnp.float32,
        )
        return jnp.exp2(gram * RATE)

    def add(k, q0, lanes, values):
        acc[k, :, pl.ds(q0, lanes)] += jnp.sum(values.reshape(-1, 8, lanes), axis=0)

    def tile(q0, lanes, r0, rows):
        ki = affinity(q0, lanes, r0, rows, IMAGE)
        kt = affinity(q0, lanes, r0, rows, TEXT)
        for k, values in enumerate((ki, kt, ki * kt)):
            add(k, q0, lanes, values)

    def work(q0, lanes, b0, blocks):
        rows = blocks * ROWS_R
        pieces = 1 if rows <= 1024 else 2
        for piece in range(pieces):
            tile(q0, lanes, b0 * ROWS_R + piece * (rows // pieces), rows // pieces)

    def work_groups(g0, groups, b0, blocks):
        for g in range(g0, g0 + groups):
            work(g * ROWS_R, ROWS_R, b0, blocks)

    early = lax.broadcasted_iota(jnp.int32, (1, ROWS_Q), 1) < HALF

    def owned(dy, dz):
        a, b = (PLACE[(h, dy, dz)] // 2 * ROWS_Q for h in "AB")
        rows = []
        for k in range(3):
            sums = acc[k, :, a : a + ROWS_Q]
            if a != b:
                sums = jnp.where(early, sums, acc[k, :, b : b + ROWS_Q])
            rows.append(jnp.sum(sums, axis=0, keepdims=True))
        return jnp.concatenate(rows + [rows[0]], axis=0)

    sum_copies = [
        pltpu.make_async_remote_copy(
            src_ref=give.at[i],
            dst_ref=take.at[i],
            send_sem=sum_send.at[i],
            recv_sem=sum_recv.at[i],
            device_id=plane(dy, dz),
            device_id_type=MESH,
        )
        for i, (dy, dz) in enumerate(SOURCES[1:])
    ]

    def hand_back(sources):
        which = [SOURCES.index(source) - 1 for source in sources]
        for i, source in zip(which, sources):
            give[i] = owned(*source)
        for i in which:
            sum_copies[i].start()

    started = 0

    def plane_upto(count):
        nonlocal started
        for i in range(started, count):
            plane_start(i)
        started = max(started, count)

    def plane_next(i):
        plane_wait(i)
        if i < len(UPTO):
            plane_upto(UPTO[i])

    loads[0].wait()
    loads[1].wait()
    project(qi, hi, ROWS_Q, IMAGE, queries)
    loads[4].wait()
    project(ri, hi, ROWS_R, IMAGE, refs)
    loads[2].wait()
    loads[3].wait()
    project(qt, ht, ROWS_Q, TEXT, queries)
    loads[5].wait()
    pl.semaphore_wait(barrier, len(greeted))
    plane_upto(2)
    project(rt, ht, ROWS_R, TEXT, refs)
    line_start(0)
    line_start(1)
    line_start(2)
    pair_copies[0].start()

    def line_next(j):
        line_wait(j)
        if j < 3:
            line_start(j + 3)
        pair_copies[j + 1].start()

    plane_next(0)
    pair_copies[0].wait_recv()
    work_groups(1, 1, 0, 2)
    line_next(0)

    plane_next(1)
    work_groups(2, 1, 0, 2)
    pair_copies[1].wait_recv()
    work_groups(1, 2, 2, 1)
    line_next(1)

    plane_next(2)
    pair_copies[2].wait_recv()
    work_groups(0, 1, 0, 4)
    work_groups(1, 2, 3, 1)
    line_next(2)

    plane_next(3)
    pair_copies[3].wait_recv()
    work_groups(3, 1, 0, 5)
    work_groups(0, 3, 4, 1)
    line_next(3)

    plane_next(4)
    pair_copies[4].wait_recv()
    work_groups(4, 1, 0, 6)
    work_groups(0, 4, 5, 1)
    line_next(4)

    plane_next(5)
    pair_copies[5].wait_recv()
    work_groups(5, 1, 0, 7)
    work_groups(0, 5, 6, 1)

    plane_next(6)
    plane_next(7)
    line_next(5)
    work_groups(6, 1, 0, 7)
    pair_copies[6].wait_recv()
    work_groups(0, 7, 7, 1)
    late = ((1, 2), (2, 1), (0, 2), (2, 0))
    soon = [source for source in SOURCES[1:] if source not in late]
    hand_back(soon)

    plane_next(8)
    plane_next(9)
    work_groups(7, 1, 0, 8)
    hand_back(late)

    total = owned(0, 0)
    for sources in (soon, late):
        for source in sources:
            i = SOURCES.index(source) - 1
            sum_copies[i].wait_recv()
            total = total + take[i]
    out_ref[...] = total

    for copies in plane_copies + line_copies:
        for copy in copies:
            copy.wait_send()
    for copy in pair_copies:
        copy.wait_send()
    for copy in sum_copies:
        copy.wait_send()


def local(query_image, query_text, ref_image, ref_text, image_head, text_head):
    count = ref_image.shape[0] * lax.axis_size("pb") * lax.axis_size("row")
    dma = pltpu.SemaphoreType.DMA
    sums = pl.pallas_call(
        kernel,
        out_shape=pltpu.VMEM((4, ROWS_Q), jnp.float32),
        in_specs=[pl.BlockSpec(memory_space=pltpu.HBM)] * 6,
        out_specs=pl.BlockSpec(memory_space=pltpu.VMEM),
        scratch_shapes=[
            pltpu.VMEM(query_image.shape, jnp.bfloat16),
            pltpu.VMEM(query_text.shape, jnp.bfloat16),
            pltpu.VMEM(ref_image.shape, jnp.bfloat16),
            pltpu.VMEM(ref_text.shape, jnp.bfloat16),
            pltpu.VMEM(image_head.shape, jnp.bfloat16),
            pltpu.VMEM(text_head.shape, jnp.bfloat16),
            pltpu.VMEM((16 * ROWS_Q, 2 * E), jnp.bfloat16),
            pltpu.VMEM((8 * ROWS_R, 2 * E), jnp.bfloat16),
            pltpu.VMEM((3, 8, 16 * ROWS_Q), jnp.float32),
            pltpu.VMEM((15, 4, ROWS_Q), jnp.float32),
            pltpu.VMEM((15, 4, ROWS_Q), jnp.float32),
            dma((6,)),
            dma((4, 10)),
            dma((4, 10)),
            dma((2, 6)),
            dma((2, 6)),
            dma((7,)),
            dma((7,)),
            dma((15,)),
            dma((15,)),
        ],
        compiler_params=pltpu.CompilerParams(
            collective_id=0, has_side_effects=True, vmem_limit_bytes=63 * 2**20
        ),
    )(query_image, query_text, ref_image, ref_text, image_head, text_head)
    return jnp.log(sums[2]) - jnp.log(sums[0]) - jnp.log(sums[1]) + jnp.log(jnp.float32(count))


def solution(mesh):
    split = P(("pb", "row"), None)
    return jax.shard_map(
        local,
        mesh=mesh,
        in_specs=(split, split, split, split, P(), P()),
        out_specs=P(("pb", "row")),
        check_vma=False,
    )
```

```python
import functools

import jax
import jax.numpy as jnp
from jax import lax
from jax.experimental import pallas as pl
from jax.experimental.pallas import tpu as pltpu
from jax.sharding import PartitionSpec as P

MESH = pl.DeviceIdType.MESH
EPS = 1e-05
RATE = 10.0 * 1.4426950408889634
E = 768
ROWS_Q = 128
ROWS_R = 256
HALF = 64
N = 4
NT = (((1,), (1,)), ((), ()))

COLUMNS = (
    ((0, 0), (0, 0), (0, 0), (0, 0)),
    ((2, 0), (2, 0), (0, 2), (0, 2)),
    ((-1, 0), (-1, 0), (0, -1), (0, -1)),
    ((1, 0), (1, 0), (0, 1), (0, 1)),
    ((0, -1), (0, -1), (-1, 0), (-1, 0)),
    ((0, 1), (0, 1), (1, 0), (1, 0)),
    ((-1, -1), (-1, -1), (-1, -1), (-1, -1)),
    ((-1, 1), (-1, 1), (1, -1), (1, -1)),
    ((2, -1), (2, -1), (-1, 2), (-1, 2)),
    ((2, 1), (2, 1), (1, 2), (1, 2)),
    ((1, -1), (1, 1), (-1, 1), (1, 1)),
    ((1, 2), (1, 2), (2, 1), (2, 1)),
    ((-1, 2), (-1, 2), (2, -1), (2, -1)),
    ((2, 2), (2, 2), (2, 2), (2, 2)),
    ((0, 2), (0, 2), (2, 0), (2, 0)),
    ((1, 1), (1, -1), (1, 1), (-1, 1)),
)
QUARTER = 32
PLACE = {("AABB"[q], q % 2, *source): 4 * i + q for i, column in enumerate(COLUMNS) for q, source in enumerate(column)}
SOURCES = tuple((dy, dz) for dy in (0, 1, -1, 2) for dz in (0, 1, -1, 2))
PLANE_DIRS = ((1, 0), (-1, 0), (0, 1), (0, -1))


def wrap(d):
    return (d + 1) % N - 1


IMAGE, TEXT = slice(0, E), slice(E, 2 * E)


def plane_items(direction):
    s = sum(direction)
    h = 0 if s > 0 else 1
    items = (
        ("A", 0, 0, None),
        ("B", 0, 0, None),
        ("A", -s, 0, h),
        ("B", 0, 1, h),
        ("B", 0, -1, None),
        ("B", 0, 2, None),
        ("B", -s, 1, h),
        ("B", -s, -1, h),
        ("B", -s, 2, h),
        ("B", -s, 0, h),
        ("B", -2 * s, 1, h),
    )
    if direction[0]:
        return items
    return tuple(("AB"["BA".index(half)], dz, dy, part) for half, dy, dz, part in items)


UPTO = (5, 5, 6, 7, 8, 10, 11)


def query_rows(half, dy, dz, part):
    start = PLACE[(half, part or 0, wrap(dy), wrap(dz))] * QUARTER
    return start, HALF if part is None else QUARTER


def device_at(x, y, z, c):
    return ((y % 2) * N + x, z * 4 + (y // 2) * 2 + c)


def unit(values):
    scale = lax.rsqrt(jnp.mean(values * values, axis=-1, keepdims=True) + EPS)
    return values * scale * E ** (-0.5)


def kernel(
    qi_hbm, qt_hbm, ri_hbm, rt_hbm, hi_hbm, ht_hbm, out_ref,
    qi, qt, ri, rt, hi, ht, queries, refs, acc, give, take,
    load_sem, plane_send, plane_recv, line_send, line_recv, pair_send, pair_recv, sum_send, sum_recv,
):
    pb, row = lax.axis_index("pb"), lax.axis_index("row")
    x, y = pb % N, (row // 2) % 2 * 2 + pb // N
    z, c = row // 4, row % 2

    def plane(dy, dz):
        return device_at(x, (y + dy + N) % N, (z + dz + N) % N, c)

    def line(dx):
        return device_at((x + dx + N) % N, y, z, c)

    pair = device_at(x, y, z, 1 - c)

    loads = []
    for i, (src, dst) in enumerate(
        (
            (qi_hbm, qi),
            (hi_hbm, hi),
            (qt_hbm, qt),
            (ht_hbm, ht),
            (ri_hbm, ri),
            (rt_hbm, rt),
        )
    ):
        copy = pltpu.make_async_copy(src, dst, load_sem.at[i])
        copy.start()
        loads.append(copy)

    barrier = pltpu.get_barrier_semaphore()
    greeted = [plane(dy, dz) for dy, dz in PLANE_DIRS] + [line(1), line(-1), pair]
    for device in greeted:
        pl.semaphore_signal(barrier, inc=1, device_id=device, device_id_type=MESH)

    acc[...] = jnp.zeros_like(acc)

    def project(features, head, rows, columns, into):
        made = unit(jnp.dot(features[...], head[...], preferred_element_type=jnp.float32))
        into[0:rows, columns] = made.astype(jnp.bfloat16)

    plane_copies = []
    for k, direction in enumerate(PLANE_DIRS):
        copies = []
        for i, (half, dy, dz, part) in enumerate(plane_items(direction)):
            start, rows = query_rows(half, dy, dz, part)
            there, _ = query_rows(half, dy - direction[0], dz - direction[1], part)
            copies.append(
                pltpu.make_async_remote_copy(
                    src_ref=queries.at[pl.ds(start, rows)],
                    dst_ref=queries.at[pl.ds(there, rows)],
                    send_sem=plane_send.at[k, i],
                    recv_sem=plane_recv.at[k, i],
                    device_id=plane(*direction),
                    device_id_type=MESH,
                )
            )
        plane_copies.append(copies)

    line_copies = []
    for k, dx in enumerate((1, -1)):
        copies = []
        for j in range(6):
            if j < 4:
                start = ((j + 2 * k) % 4) * HALF
            else:
                start = (2 + j - 4) * ROWS_R + k * HALF
            there = (2 + j) * ROWS_R + k * HALF
            copies.append(
                pltpu.make_async_remote_copy(
                    src_ref=refs.at[pl.ds(start, HALF)],
                    dst_ref=refs.at[pl.ds(there, HALF)],
                    send_sem=line_send.at[k, j],
                    recv_sem=line_recv.at[k, j],
                    device_id=line(dx),
                    device_id_type=MESH,
                )
            )
        line_copies.append(copies)
    pair_copies = []
    for j in range(7):
        start = (1 + j) * ROWS_R if j else 0
        there = start + 2 * HALF if j else ROWS_R
        rows = 2 * HALF if j else ROWS_R
        pair_copies.append(
            pltpu.make_async_remote_copy(
                src_ref=refs.at[pl.ds(start, rows)],
                dst_ref=refs.at[pl.ds(there, rows)],
                send_sem=pair_send.at[j],
                recv_sem=pair_recv.at[j],
                device_id=pair,
                device_id_type=MESH,
            )
        )

    def plane_start(i):
        for copies in plane_copies:
            copies[i].start()

    def plane_wait(i):
        for copies in plane_copies:
            copies[i].wait_recv()

    def line_start(j):
        for copies in line_copies:
            copies[j].start()

    def line_wait(j):
        for copies in line_copies:
            copies[j].wait_recv()

    def affinity(q0, lanes, r0, rows, columns):
        gram = lax.dot_general(
            refs[pl.ds(r0, rows), columns],
            queries[pl.ds(q0, lanes), columns],
            NT,
            preferred_element_type=jnp.float32,
        )
        return jnp.exp2(gram * RATE)

    def add(k, q0, lanes, values):
        acc[k, :, pl.ds(q0, lanes)] += jnp.sum(values.reshape(-1, 8, lanes), axis=0)

    def tile(q0, lanes, r0, rows):
        ki = affinity(q0, lanes, r0, rows, IMAGE)
        kt = affinity(q0, lanes, r0, rows, TEXT)
        for k, values in enumerate((ki, kt, ki * kt)):
            add(k, q0, lanes, values)

    def work(q0, lanes, b0, blocks):
        rows = blocks * ROWS_R
        pieces = 1 if rows <= 1024 else 2
        for piece in range(pieces):
            tile(q0, lanes, b0 * ROWS_R + piece * (rows // pieces), rows // pieces)

    def work_groups(g0, groups, b0, blocks):
        for g in range(g0, g0 + groups):
            work(g * ROWS_R, ROWS_R, b0, blocks)

    quarter = lax.broadcasted_iota(jnp.int32, (1, ROWS_Q), 1) // QUARTER

    def owned(dy, dz):
        places = [PLACE[(half, part, dy, dz)] // 4 * ROWS_Q for half in "AB" for part in range(2)]
        rows = []
        for k in range(3):
            sums = acc[k, :, places[0] : places[0] + ROWS_Q]
            for q in range(1, 4):
                if places[q] != places[q - 1]:
                    sums = jnp.where(quarter < q, sums, acc[k, :, places[q] : places[q] + ROWS_Q])
            rows.append(jnp.sum(sums, axis=0, keepdims=True))
        return jnp.concatenate(rows + [rows[0]], axis=0)

    sum_copies = [
        pltpu.make_async_remote_copy(
            src_ref=give.at[i],
            dst_ref=take.at[i],
            send_sem=sum_send.at[i],
            recv_sem=sum_recv.at[i],
            device_id=plane(dy, dz),
            device_id_type=MESH,
        )
        for i, (dy, dz) in enumerate(SOURCES[1:])
    ]

    def hand_back(sources):
        which = [SOURCES.index(source) - 1 for source in sources]
        for i, source in zip(which, sources):
            give[i] = owned(*source)
        for i in which:
            sum_copies[i].start()

    started = 0

    def plane_upto(count):
        nonlocal started
        for i in range(started, count):
            plane_start(i)
        started = max(started, count)

    def plane_next(i):
        plane_wait(i)
        if i < len(UPTO):
            plane_upto(UPTO[i])

    loads[0].wait()
    loads[1].wait()
    project(qi, hi, ROWS_Q, IMAGE, queries)
    loads[2].wait()
    loads[3].wait()
    project(qt, ht, ROWS_Q, TEXT, queries)
    pl.semaphore_wait(barrier, len(greeted))
    plane_upto(2)
    loads[4].wait()
    project(ri, hi, ROWS_R, IMAGE, refs)
    loads[5].wait()
    project(rt, ht, ROWS_R, TEXT, refs)
    line_start(0)
    line_start(1)
    line_start(2)
    late = ((2, 0), (0, 2), (1, 1), (1, -1), (-1, 1))
    soon = [source for source in SOURCES[1:] if source not in late]

    pair_copies[0].start()

    def line_next(j):
        line_wait(j)
        if j < 3:
            line_start(j + 3)
        pair_copies[j + 1].start()

    plane_next(0)
    pair_copies[0].wait_recv()
    work_groups(1, 1, 0, 2)
    line_next(0)

    plane_next(1)
    work_groups(2, 1, 0, 2)
    pair_copies[1].wait_recv()
    work_groups(1, 2, 2, 1)
    line_next(1)

    plane_next(2)
    pair_copies[2].wait_recv()
    work_groups(0, 1, 0, 4)
    work_groups(1, 2, 3, 1)
    line_next(2)

    plane_next(3)
    plane_next(4)
    pair_copies[3].wait_recv()
    work_groups(3, 1, 0, 5)
    work_groups(0, 3, 4, 1)
    line_next(3)

    plane_next(5)
    pair_copies[4].wait_recv()
    work_groups(4, 1, 0, 6)
    work_groups(0, 4, 5, 1)
    line_next(4)

    plane_next(6)
    pair_copies[5].wait_recv()
    work_groups(5, 1, 0, 7)
    work_groups(0, 5, 6, 1)

    line_next(5)
    plane_next(7)
    plane_next(8)
    work_groups(6, 1, 0, 7)
    pair_copies[6].wait_recv()
    work_groups(0, 7, 7, 1)
    hand_back(soon)

    plane_next(9)
    plane_next(10)
    work_groups(7, 1, 0, 8)
    hand_back(late)

    total = owned(0, 0)
    for sources in (soon, late):
        for source in sources:
            i = SOURCES.index(source) - 1
            sum_copies[i].wait_recv()
            total = total + take[i]
    out_ref[...] = total

    for copies in plane_copies + line_copies:
        for copy in copies:
            copy.wait_send()
    for copy in pair_copies:
        copy.wait_send()
    for copy in sum_copies:
        copy.wait_send()


def local(query_image, query_text, ref_image, ref_text, image_head, text_head):
    count = ref_image.shape[0] * lax.axis_size("pb") * lax.axis_size("row")
    dma = pltpu.SemaphoreType.DMA
    sums = pl.pallas_call(
        kernel,
        out_shape=pltpu.VMEM((4, ROWS_Q), jnp.float32),
        in_specs=[pl.BlockSpec(memory_space=pltpu.HBM)] * 6,
        out_specs=pl.BlockSpec(memory_space=pltpu.VMEM),
        scratch_shapes=[
            pltpu.VMEM(query_image.shape, jnp.bfloat16),
            pltpu.VMEM(query_text.shape, jnp.bfloat16),
            pltpu.VMEM(ref_image.shape, jnp.bfloat16),
            pltpu.VMEM(ref_text.shape, jnp.bfloat16),
            pltpu.VMEM(image_head.shape, jnp.bfloat16),
            pltpu.VMEM(text_head.shape, jnp.bfloat16),
            pltpu.VMEM((16 * ROWS_Q, 2 * E), jnp.bfloat16),
            pltpu.VMEM((8 * ROWS_R, 2 * E), jnp.bfloat16),
            pltpu.VMEM((3, 8, 16 * ROWS_Q), jnp.float32),
            pltpu.VMEM((15, 4, ROWS_Q), jnp.float32),
            pltpu.VMEM((15, 4, ROWS_Q), jnp.float32),
            dma((6,)),
            dma((4, 11)),
            dma((4, 11)),
            dma((2, 6)),
            dma((2, 6)),
            dma((7,)),
            dma((7,)),
            dma((15,)),
            dma((15,)),
        ],
        compiler_params=pltpu.CompilerParams(
            collective_id=0, has_side_effects=True, vmem_limit_bytes=63 * 2**20
        ),
    )(query_image, query_text, ref_image, ref_text, image_head, text_head)
    return jnp.log(sums[2]) - jnp.log(sums[0]) - jnp.log(sums[1]) + jnp.log(jnp.float32(count))


def solution(mesh):
    split = P(("pb", "row"), None)
    return jax.shard_map(
        local,
        mesh=mesh,
        in_specs=(split, split, split, split, P(), P()),
        out_specs=P(("pb", "row")),
        check_vma=False,
    )
```

```python
import functools

import jax
import jax.numpy as jnp
from jax import lax
from jax.experimental import pallas as pl
from jax.experimental.pallas import tpu as pltpu
from jax.sharding import PartitionSpec as P

MESH = pl.DeviceIdType.MESH
EPS = 1e-05
RATE = 10.0 * 1.4426950408889634
E = 768
ROWS_Q = 128
ROWS_R = 256
HALF = 64
N = 4
NT = (((1,), (1,)), ((), ()))

COLUMNS = (
    ((0, 0), (0, 0), (0, 0), (0, 0)),
    ((2, 0), (2, 0), (0, 2), (0, 2)),
    ((-1, 0), (-1, 0), (0, -1), (0, -1)),
    ((1, 0), (1, 0), (0, 1), (0, 1)),
    ((0, -1), (0, -1), (-1, 0), (-1, 0)),
    ((0, 1), (0, 1), (1, 0), (1, 0)),
    ((-1, -1), (-1, -1), (-1, -1), (-1, -1)),
    ((-1, 1), (-1, 1), (1, -1), (1, -1)),
    ((2, -1), (2, -1), (-1, 2), (-1, 2)),
    ((2, 1), (2, 1), (1, 2), (1, 2)),
    ((1, -1), (1, 1), (-1, 1), (1, 1)),
    ((1, 2), (1, 2), (2, 1), (2, 1)),
    ((-1, 2), (-1, 2), (2, -1), (2, -1)),
    ((2, 2), (2, 2), (2, 2), (2, 2)),
    ((0, 2), (0, 2), (2, 0), (2, 0)),
    ((1, 1), (1, -1), (1, 1), (-1, 1)),
)
QUARTER = 32
PLACE = {("AABB"[q], q % 2, *source): 4 * i + q for i, column in enumerate(COLUMNS) for q, source in enumerate(column)}
SOURCES = tuple((dy, dz) for dy in (0, 1, -1, 2) for dz in (0, 1, -1, 2))
PLANE_DIRS = ((1, 0), (-1, 0), (0, 1), (0, -1))


def wrap(d):
    return (d + 1) % N - 1


IMAGE, TEXT = slice(0, E), slice(E, 2 * E)


def plane_items(direction):
    s = sum(direction)
    h = 0 if s > 0 else 1
    items = (
        ("A", 0, 0, None),
        ("B", 0, 0, None),
        ("A", -s, 0, h),
        ("B", 0, 1, h),
        ("B", 0, -1, None),
        ("B", 0, 2, None),
        ("B", -s, 1, h),
        ("B", -s, -1, h),
        ("B", -s, 2, h),
        ("B", -s, 0, h),
        ("B", -2 * s, 1, h),
    )
    if direction[0]:
        return items
    return tuple(("AB"["BA".index(half)], dz, dy, part) for half, dy, dz, part in items)


UPTO = (5, 5, 6, 7, 8, 10, 11)


def query_rows(half, dy, dz, part):
    start = PLACE[(half, part or 0, wrap(dy), wrap(dz))] * QUARTER
    return start, HALF if part is None else QUARTER


def device_at(x, y, z, c):
    return ((y % 2) * N + x, z * 4 + (y // 2) * 2 + c)


def unit(values):
    scale = lax.rsqrt(jnp.mean(values * values, axis=-1, keepdims=True) + EPS)
    return values * scale * E ** (-0.5)


def kernel(
    qi_hbm, qt_hbm, ri_hbm, rt_hbm, hi_hbm, ht_hbm, out_ref,
    qi, qt, ri, rt, hi, ht, queries, refs, acc, give, take,
    load_sem, plane_send, plane_recv, line_send, line_recv, pair_send, pair_recv, sum_send, sum_recv,
):
    pb, row = lax.axis_index("pb"), lax.axis_index("row")
    x, y = pb % N, (row // 2) % 2 * 2 + pb // N
    z, c = row // 4, row % 2

    def plane(dy, dz):
        return device_at(x, (y + dy + N) % N, (z + dz + N) % N, c)

    def line(dx):
        return device_at((x + dx + N) % N, y, z, c)

    pair = device_at(x, y, z, 1 - c)

    def halves(src, dst):
        rows = src.shape[0] // 2
        return [(src.at[pl.ds(p * rows, rows)], dst.at[pl.ds(p * rows, rows)]) for p in range(2)]

    loads = []
    for i, (src, dst) in enumerate(
        (
            (qi_hbm, qi),
            *halves(hi_hbm, hi),
            (qt_hbm, qt),
            *halves(ht_hbm, ht),
            (ri_hbm, ri),
            (rt_hbm, rt),
        )
    ):
        copy = pltpu.make_async_copy(src, dst, load_sem.at[i])
        copy.start()
        loads.append(copy)

    barrier = pltpu.get_barrier_semaphore()
    greeted = [plane(dy, dz) for dy, dz in PLANE_DIRS] + [line(1), line(-1), pair]
    for device in greeted:
        pl.semaphore_signal(barrier, inc=1, device_id=device, device_id_type=MESH)

    acc[...] = jnp.zeros_like(acc)

    def project(features, head, rows, columns, into, needs):
        depth = head.shape[0] // 2
        made = 0.0
        for p in range(2):
            for n in needs[p]:
                loads[n].wait()
            part = slice(p * depth, (p + 1) * depth)
            made += jnp.dot(features[:, part], head[part, :], preferred_element_type=jnp.float32)
        made = unit(made)
        into[0:rows, columns] = made.astype(jnp.bfloat16)

    plane_copies = []
    for k, direction in enumerate(PLANE_DIRS):
        copies = []
        for i, (half, dy, dz, part) in enumerate(plane_items(direction)):
            start, rows = query_rows(half, dy, dz, part)
            there, _ = query_rows(half, dy - direction[0], dz - direction[1], part)
            copies.append(
                pltpu.make_async_remote_copy(
                    src_ref=queries.at[pl.ds(start, rows)],
                    dst_ref=queries.at[pl.ds(there, rows)],
                    send_sem=plane_send.at[k, i],
                    recv_sem=plane_recv.at[k, i],
                    device_id=plane(*direction),
                    device_id_type=MESH,
                )
            )
        plane_copies.append(copies)

    line_copies = []
    for k, dx in enumerate((1, -1)):
        copies = []
        for j in range(6):
            if j < 4:
                start = ((j + 2 * k) % 4) * HALF
            else:
                start = (2 + j - 4) * ROWS_R + k * HALF
            there = (2 + j) * ROWS_R + k * HALF
            copies.append(
                pltpu.make_async_remote_copy(
                    src_ref=refs.at[pl.ds(start, HALF)],
                    dst_ref=refs.at[pl.ds(there, HALF)],
                    send_sem=line_send.at[k, j],
                    recv_sem=line_recv.at[k, j],
                    device_id=line(dx),
                    device_id_type=MESH,
                )
            )
        line_copies.append(copies)
    pair_copies = []
    for j in range(7):
        start = (1 + j) * ROWS_R if j else 0
        there = start + 2 * HALF if j else ROWS_R
        rows = 2 * HALF if j else ROWS_R
        pair_copies.append(
            pltpu.make_async_remote_copy(
                src_ref=refs.at[pl.ds(start, rows)],
                dst_ref=refs.at[pl.ds(there, rows)],
                send_sem=pair_send.at[j],
                recv_sem=pair_recv.at[j],
                device_id=pair,
                device_id_type=MESH,
            )
        )

    def plane_start(i):
        for copies in plane_copies:
            copies[i].start()

    def plane_wait(i):
        for copies in plane_copies:
            copies[i].wait_recv()

    def line_start(j):
        for copies in line_copies:
            copies[j].start()

    def line_wait(j):
        for copies in line_copies:
            copies[j].wait_recv()

    def affinity(q0, lanes, r0, rows, columns):
        gram = lax.dot_general(
            refs[pl.ds(r0, rows), columns],
            queries[pl.ds(q0, lanes), columns],
            NT,
            preferred_element_type=jnp.float32,
        )
        return jnp.exp2(gram * RATE)

    def add(k, q0, lanes, values):
        acc[k, :, pl.ds(q0, lanes)] += jnp.sum(values.reshape(-1, 8, lanes), axis=0)

    def tile(q0, lanes, r0, rows):
        ki = affinity(q0, lanes, r0, rows, IMAGE)
        kt = affinity(q0, lanes, r0, rows, TEXT)
        for k, values in enumerate((ki, kt, ki * kt)):
            add(k, q0, lanes, values)

    def work(q0, lanes, b0, blocks):
        rows = blocks * ROWS_R
        pieces = 1 if rows <= 1024 else 2
        for piece in range(pieces):
            tile(q0, lanes, b0 * ROWS_R + piece * (rows // pieces), rows // pieces)

    def work_groups(g0, groups, b0, blocks):
        for g in range(g0, g0 + groups):
            work(g * ROWS_R, ROWS_R, b0, blocks)

    quarter = lax.broadcasted_iota(jnp.int32, (1, ROWS_Q), 1) // QUARTER

    def owned(dy, dz):
        places = [PLACE[(half, part, dy, dz)] // 4 * ROWS_Q for half in "AB" for part in range(2)]
        rows = []
        for k in range(3):
            sums = acc[k, :, places[0] : places[0] + ROWS_Q]
            for q in range(1, 4):
                if places[q] != places[q - 1]:
                    sums = jnp.where(quarter < q, sums, acc[k, :, places[q] : places[q] + ROWS_Q])
            rows.append(jnp.sum(sums, axis=0, keepdims=True))
        return jnp.concatenate(rows + [rows[0]], axis=0)

    sum_copies = [
        pltpu.make_async_remote_copy(
            src_ref=give.at[i],
            dst_ref=take.at[i],
            send_sem=sum_send.at[i],
            recv_sem=sum_recv.at[i],
            device_id=plane(dy, dz),
            device_id_type=MESH,
        )
        for i, (dy, dz) in enumerate(SOURCES[1:])
    ]

    def hand_back(sources):
        which = [SOURCES.index(source) - 1 for source in sources]
        for i, source in zip(which, sources):
            give[i] = owned(*source)
        for i in which:
            sum_copies[i].start()

    started = 0

    def plane_upto(count):
        nonlocal started
        for i in range(started, count):
            plane_start(i)
        started = max(started, count)

    def plane_next(i):
        plane_wait(i)
        if i < len(UPTO):
            plane_upto(UPTO[i])

    project(qi, hi, ROWS_Q, IMAGE, queries, ((0, 1), (2,)))
    project(qt, ht, ROWS_Q, TEXT, queries, ((3, 4), (5,)))
    pl.semaphore_wait(barrier, len(greeted))
    plane_upto(2)
    project(ri, hi, ROWS_R, IMAGE, refs, ((6,), ()))
    project(rt, ht, ROWS_R, TEXT, refs, ((7,), ()))
    line_start(0)
    line_start(1)
    line_start(2)
    late = ((2, 0), (0, 2), (1, 1), (1, -1), (-1, 1))
    soon = [source for source in SOURCES[1:] if source not in late]

    pair_copies[0].start()

    def line_next(j):
        line_wait(j)
        if j < 3:
            line_start(j + 3)
        pair_copies[j + 1].start()

    plane_next(0)
    pair_copies[0].wait_recv()
    work_groups(1, 1, 0, 2)
    line_next(0)

    plane_next(1)
    work_groups(2, 1, 0, 2)
    pair_copies[1].wait_recv()
    work_groups(1, 2, 2, 1)
    line_next(1)

    plane_next(2)
    pair_copies[2].wait_recv()
    work_groups(0, 1, 0, 4)
    work_groups(1, 2, 3, 1)
    line_next(2)

    plane_next(3)
    plane_next(4)
    pair_copies[3].wait_recv()
    work_groups(3, 1, 0, 5)
    work_groups(0, 3, 4, 1)
    line_next(3)

    plane_next(5)
    pair_copies[4].wait_recv()
    work_groups(4, 1, 0, 6)
    work_groups(0, 4, 5, 1)
    line_next(4)

    plane_next(6)
    pair_copies[5].wait_recv()
    work_groups(5, 1, 0, 7)
    work_groups(0, 5, 6, 1)

    line_next(5)
    plane_next(7)
    plane_next(8)
    work_groups(6, 1, 0, 7)
    pair_copies[6].wait_recv()
    work_groups(0, 7, 7, 1)
    hand_back(soon)

    plane_next(9)
    plane_next(10)
    work_groups(7, 1, 0, 8)
    hand_back(late)

    total = owned(0, 0)
    for sources in (soon, late):
        for source in sources:
            i = SOURCES.index(source) - 1
            sum_copies[i].wait_recv()
            total = total + take[i]
    out_ref[...] = total

    for copies in plane_copies + line_copies:
        for copy in copies:
            copy.wait_send()
    for copy in pair_copies:
        copy.wait_send()
    for copy in sum_copies:
        copy.wait_send()


def local(query_image, query_text, ref_image, ref_text, image_head, text_head):
    count = ref_image.shape[0] * lax.axis_size("pb") * lax.axis_size("row")
    dma = pltpu.SemaphoreType.DMA
    sums = pl.pallas_call(
        kernel,
        out_shape=pltpu.VMEM((4, ROWS_Q), jnp.float32),
        in_specs=[pl.BlockSpec(memory_space=pltpu.HBM)] * 6,
        out_specs=pl.BlockSpec(memory_space=pltpu.VMEM),
        scratch_shapes=[
            pltpu.VMEM(query_image.shape, jnp.bfloat16),
            pltpu.VMEM(query_text.shape, jnp.bfloat16),
            pltpu.VMEM(ref_image.shape, jnp.bfloat16),
            pltpu.VMEM(ref_text.shape, jnp.bfloat16),
            pltpu.VMEM(image_head.shape, jnp.bfloat16),
            pltpu.VMEM(text_head.shape, jnp.bfloat16),
            pltpu.VMEM((16 * ROWS_Q, 2 * E), jnp.bfloat16),
            pltpu.VMEM((8 * ROWS_R, 2 * E), jnp.bfloat16),
            pltpu.VMEM((3, 8, 16 * ROWS_Q), jnp.float32),
            pltpu.VMEM((15, 4, ROWS_Q), jnp.float32),
            pltpu.VMEM((15, 4, ROWS_Q), jnp.float32),
            dma((8,)),
            dma((4, 11)),
            dma((4, 11)),
            dma((2, 6)),
            dma((2, 6)),
            dma((7,)),
            dma((7,)),
            dma((15,)),
            dma((15,)),
        ],
        compiler_params=pltpu.CompilerParams(
            collective_id=0, has_side_effects=True, vmem_limit_bytes=63 * 2**20
        ),
    )(query_image, query_text, ref_image, ref_text, image_head, text_head)
    return jnp.log(sums[2]) - jnp.log(sums[0]) - jnp.log(sums[1]) + jnp.log(jnp.float32(count))


def solution(mesh):
    split = P(("pb", "row"), None)
    return jax.shard_map(
        local,
        mesh=mesh,
        in_specs=(split, split, split, split, P(), P()),
        out_specs=P(("pb", "row")),
        check_vma=False,
    )
```

```python
import functools

import jax
import jax.numpy as jnp
from jax import lax
from jax.experimental import pallas as pl
from jax.experimental.pallas import tpu as pltpu
from jax.sharding import PartitionSpec as P

MESH = pl.DeviceIdType.MESH
EPS = 1e-05
RATE = 10.0 * 1.4426950408889634
E = 768
ROWS_Q = 128
ROWS_R = 256
HALF = 64
N = 4
NT = (((1,), (1,)), ((), ()))

COLUMNS = (
    ((0, 0), (0, 0), (0, 0), (0, 0)),
    ((2, 0), (2, 0), (0, 2), (0, 2)),
    ((-1, 0), (-1, 0), (0, -1), (0, -1)),
    ((1, 0), (1, 0), (0, 1), (0, 1)),
    ((0, -1), (0, -1), (-1, 0), (-1, 0)),
    ((0, 1), (0, 1), (1, 0), (1, 0)),
    ((-1, -1), (-1, -1), (-1, -1), (-1, -1)),
    ((-1, 1), (-1, 1), (1, -1), (1, -1)),
    ((2, -1), (2, -1), (-1, 2), (-1, 2)),
    ((2, 1), (2, 1), (1, 2), (1, 2)),
    ((1, -1), (1, 1), (-1, 1), (1, 1)),
    ((1, 2), (1, 2), (2, 1), (2, 1)),
    ((-1, 2), (-1, 2), (2, -1), (2, -1)),
    ((2, 2), (2, 2), (2, 2), (2, 2)),
    ((0, 2), (0, 2), (2, 0), (2, 0)),
    ((1, 1), (1, -1), (1, 1), (-1, 1)),
)
QUARTER = 32
PLACE = {("AABB"[q], q % 2, *source): 4 * i + q for i, column in enumerate(COLUMNS) for q, source in enumerate(column)}
SOURCES = tuple((dy, dz) for dy in (0, 1, -1, 2) for dz in (0, 1, -1, 2))
PLANE_DIRS = ((1, 0), (-1, 0), (0, 1), (0, -1))


def wrap(d):
    return (d + 1) % N - 1


IMAGE, TEXT = slice(0, E), slice(E, 2 * E)


def plane_items(direction):
    s = sum(direction)
    h = 0 if s > 0 else 1
    items = (
        ("A", 0, 0, None),
        ("B", 0, 0, None),
        ("A", -s, 0, h),
        ("B", 0, 1, h),
        ("B", 0, -1, None),
        ("B", 0, 2, None),
        ("B", -s, 1, h),
        ("B", -s, -1, h),
        ("B", -s, 2, h),
        ("B", -s, 0, h),
        ("B", -2 * s, 1, h),
    )
    if direction[0]:
        return items
    return tuple(("AB"["BA".index(half)], dz, dy, part) for half, dy, dz, part in items)


UPTO = (5, 5, 6, 7, 8, 10, 11)


def query_rows(half, dy, dz, part):
    start = PLACE[(half, part or 0, wrap(dy), wrap(dz))] * QUARTER
    return start, HALF if part is None else QUARTER


def device_at(x, y, z, c):
    return ((y % 2) * N + x, z * 4 + (y // 2) * 2 + c)


def unit(values):
    scale = lax.rsqrt(jnp.mean(values * values, axis=-1, keepdims=True) + EPS)
    return values * scale * E ** (-0.5)


def kernel(
    qi_hbm, qt_hbm, ri_hbm, rt_hbm, hi_hbm, ht_hbm, out_ref,
    qi, qt, ri, rt, hi, ht, queries, refs, acc, give, take,
    load_sem, plane_send, plane_recv, line_send, line_recv, pair_send, pair_recv, sum_send, sum_recv,
):
    pb, row = lax.axis_index("pb"), lax.axis_index("row")
    x, y = pb % N, (row // 2) % 2 * 2 + pb // N
    z, c = row // 4, row % 2

    def plane(dy, dz):
        return device_at(x, (y + dy + N) % N, (z + dz + N) % N, c)

    def line(dx):
        return device_at((x + dx + N) % N, y, z, c)

    pair = device_at(x, y, z, 1 - c)

    loads = []
    for i, (src, dst) in enumerate(
        (
            (qi_hbm, qi),
            (hi_hbm, hi),
            (qt_hbm, qt),
            (ht_hbm, ht),
            (ri_hbm, ri),
            (rt_hbm, rt),
        )
    ):
        copy = pltpu.make_async_copy(src, dst, load_sem.at[i])
        copy.start()
        loads.append(copy)

    barrier = pltpu.get_barrier_semaphore()
    greeted = [plane(dy, dz) for dy, dz in PLANE_DIRS] + [line(1), line(-1), pair]
    for device in greeted:
        pl.semaphore_signal(barrier, inc=1, device_id=device, device_id_type=MESH)

    acc[...] = jnp.zeros_like(acc)

    def project(features, head, rows, columns, into):
        made = unit(jnp.dot(features[...], head[...], preferred_element_type=jnp.float32))
        into[0:rows, columns] = made.astype(jnp.bfloat16)

    plane_copies = []
    for k, direction in enumerate(PLANE_DIRS):
        copies = []
        for i, (half, dy, dz, part) in enumerate(plane_items(direction)):
            start, rows = query_rows(half, dy, dz, part)
            there, _ = query_rows(half, dy - direction[0], dz - direction[1], part)
            copies.append(
                pltpu.make_async_remote_copy(
                    src_ref=queries.at[pl.ds(start, rows)],
                    dst_ref=queries.at[pl.ds(there, rows)],
                    send_sem=plane_send.at[k, i],
                    recv_sem=plane_recv.at[k, i],
                    device_id=plane(*direction),
                    device_id_type=MESH,
                )
            )
        plane_copies.append(copies)

    line_copies = []
    for k, dx in enumerate((1, -1)):
        copies = []
        for j in range(6):
            if j < 4:
                start = ((j + 2 * k) % 4) * HALF
            else:
                start = (2 + j - 4) * ROWS_R + k * HALF
            there = (2 + j) * ROWS_R + k * HALF
            copies.append(
                pltpu.make_async_remote_copy(
                    src_ref=refs.at[pl.ds(start, HALF)],
                    dst_ref=refs.at[pl.ds(there, HALF)],
                    send_sem=line_send.at[k, j],
                    recv_sem=line_recv.at[k, j],
                    device_id=line(dx),
                    device_id_type=MESH,
                )
            )
        line_copies.append(copies)
    pair_copies = []
    for j in range(7):
        start = (1 + j) * ROWS_R if j else 0
        there = start + 2 * HALF if j else ROWS_R
        rows = 2 * HALF if j else ROWS_R
        pair_copies.append(
            pltpu.make_async_remote_copy(
                src_ref=refs.at[pl.ds(start, rows)],
                dst_ref=refs.at[pl.ds(there, rows)],
                send_sem=pair_send.at[j],
                recv_sem=pair_recv.at[j],
                device_id=pair,
                device_id_type=MESH,
            )
        )

    def plane_start(i):
        for copies in plane_copies:
            copies[i].start()

    def plane_wait(i):
        for copies in plane_copies:
            copies[i].wait_recv()

    def line_start(j):
        for copies in line_copies:
            copies[j].start()

    def line_wait(j):
        for copies in line_copies:
            copies[j].wait_recv()

    def affinity(q0, lanes, r0, rows, columns):
        gram = lax.dot_general(
            refs[pl.ds(r0, rows), columns],
            queries[pl.ds(q0, lanes), columns],
            NT,
            preferred_element_type=jnp.float32,
        )
        return jnp.exp2(gram * RATE)

    def add(k, q0, lanes, values):
        acc[k, :, pl.ds(q0, lanes)] += jnp.sum(values.reshape(-1, 8, lanes), axis=0)

    def tile(q0, lanes, r0, rows):
        ki = affinity(q0, lanes, r0, rows, IMAGE)
        kt = affinity(q0, lanes, r0, rows, TEXT)
        for k, values in enumerate((ki, kt, ki * kt)):
            add(k, q0, lanes, values)

    def work(q0, lanes, b0, blocks):
        rows = blocks * ROWS_R
        pieces = 1 if rows <= 1024 else 2
        for piece in range(pieces):
            tile(q0, lanes, b0 * ROWS_R + piece * (rows // pieces), rows // pieces)

    def work_groups(g0, groups, b0, blocks):
        for g in range(g0, g0 + groups):
            work(g * ROWS_R, ROWS_R, b0, blocks)

    quarter = lax.broadcasted_iota(jnp.int32, (1, ROWS_Q), 1) // QUARTER

    def owned(dy, dz):
        places = [PLACE[(half, part, dy, dz)] // 4 * ROWS_Q for half in "AB" for part in range(2)]
        rows = []
        for k in range(3):
            sums = acc[k, :, places[0] : places[0] + ROWS_Q]
            for q in range(1, 4):
                if places[q] != places[q - 1]:
                    sums = jnp.where(quarter < q, sums, acc[k, :, places[q] : places[q] + ROWS_Q])
            rows.append(jnp.sum(sums, axis=0, keepdims=True))
        return jnp.concatenate(rows + [rows[0]], axis=0)

    sum_copies = [
        pltpu.make_async_remote_copy(
            src_ref=give.at[i],
            dst_ref=take.at[i],
            send_sem=sum_send.at[i],
            recv_sem=sum_recv.at[i],
            device_id=plane(dy, dz),
            device_id_type=MESH,
        )
        for i, (dy, dz) in enumerate(SOURCES[1:])
    ]

    def hand_back(sources):
        which = [SOURCES.index(source) - 1 for source in sources]
        for i, source in zip(which, sources):
            give[i] = owned(*source)
        for i in which:
            sum_copies[i].start()

    started = 0

    def plane_upto(count):
        nonlocal started
        for i in range(started, count):
            plane_start(i)
        started = max(started, count)

    def plane_next(i):
        plane_wait(i)
        if i < len(UPTO):
            plane_upto(UPTO[i])

    loads[0].wait()
    loads[1].wait()
    project(qi, hi, ROWS_Q, IMAGE, queries)
    loads[2].wait()
    loads[3].wait()
    project(qt, ht, ROWS_Q, TEXT, queries)
    pl.semaphore_wait(barrier, len(greeted))
    plane_upto(2)
    loads[4].wait()
    project(ri, hi, ROWS_R, IMAGE, refs)
    loads[5].wait()
    project(rt, ht, ROWS_R, TEXT, refs)
    line_start(0)
    line_start(1)
    line_start(2)
    late = ((2, 0), (0, 2), (1, 1), (1, -1), (-1, 1))
    soon = [source for source in SOURCES[1:] if source not in late]

    pair_copies[0].start()

    def line_next(j):
        line_wait(j)
        if j < 3:
            line_start(j + 3)
        pair_copies[j + 1].start()

    plane_next(0)
    pair_copies[0].wait_recv()
    work_groups(1, 1, 0, 2)
    line_next(0)

    plane_next(1)
    work_groups(2, 1, 0, 2)
    pair_copies[1].wait_recv()
    work_groups(1, 2, 2, 1)
    line_next(1)

    plane_next(2)
    pair_copies[2].wait_recv()
    work_groups(0, 1, 0, 4)
    work_groups(1, 2, 3, 1)
    line_next(2)

    plane_next(3)
    plane_next(4)
    pair_copies[3].wait_recv()
    work_groups(3, 1, 0, 5)
    work_groups(0, 3, 4, 1)
    line_next(3)

    plane_next(5)
    pair_copies[4].wait_recv()
    work_groups(4, 1, 0, 6)
    work_groups(0, 4, 5, 1)
    line_next(4)

    plane_next(6)
    pair_copies[5].wait_recv()
    work_groups(5, 1, 0, 7)
    work_groups(0, 5, 6, 1)

    line_next(5)
    plane_next(7)
    plane_next(8)
    work_groups(6, 1, 0, 7)
    pair_copies[6].wait_recv()
    work_groups(0, 7, 7, 1)
    hand_back(soon)
    total = owned(0, 0)

    plane_next(9)
    plane_next(10)
    work_groups(7, 1, 0, 8)
    hand_back(late)

    for sources in (soon, late):
        for source in sources:
            i = SOURCES.index(source) - 1
            sum_copies[i].wait_recv()
            total = total + take[i]
    out_ref[...] = total

    for copies in plane_copies + line_copies:
        for copy in copies:
            copy.wait_send()
    for copy in pair_copies:
        copy.wait_send()
    for copy in sum_copies:
        copy.wait_send()


def local(query_image, query_text, ref_image, ref_text, image_head, text_head):
    count = ref_image.shape[0] * lax.axis_size("pb") * lax.axis_size("row")
    dma = pltpu.SemaphoreType.DMA
    sums = pl.pallas_call(
        kernel,
        out_shape=pltpu.VMEM((4, ROWS_Q), jnp.float32),
        in_specs=[pl.BlockSpec(memory_space=pltpu.HBM)] * 6,
        out_specs=pl.BlockSpec(memory_space=pltpu.VMEM),
        scratch_shapes=[
            pltpu.VMEM(query_image.shape, jnp.bfloat16),
            pltpu.VMEM(query_text.shape, jnp.bfloat16),
            pltpu.VMEM(ref_image.shape, jnp.bfloat16),
            pltpu.VMEM(ref_text.shape, jnp.bfloat16),
            pltpu.VMEM(image_head.shape, jnp.bfloat16),
            pltpu.VMEM(text_head.shape, jnp.bfloat16),
            pltpu.VMEM((16 * ROWS_Q, 2 * E), jnp.bfloat16),
            pltpu.VMEM((8 * ROWS_R, 2 * E), jnp.bfloat16),
            pltpu.VMEM((3, 8, 16 * ROWS_Q), jnp.float32),
            pltpu.VMEM((15, 4, ROWS_Q), jnp.float32),
            pltpu.VMEM((15, 4, ROWS_Q), jnp.float32),
            dma((6,)),
            dma((4, 11)),
            dma((4, 11)),
            dma((2, 6)),
            dma((2, 6)),
            dma((7,)),
            dma((7,)),
            dma((15,)),
            dma((15,)),
        ],
        compiler_params=pltpu.CompilerParams(
            collective_id=0, has_side_effects=True, vmem_limit_bytes=63 * 2**20
        ),
    )(query_image, query_text, ref_image, ref_text, image_head, text_head)
    return jnp.log(sums[2]) - jnp.log(sums[0]) - jnp.log(sums[1]) + jnp.log(jnp.float32(count))


def solution(mesh):
    split = P(("pb", "row"), None)
    return jax.shard_map(
        local,
        mesh=mesh,
        in_specs=(split, split, split, split, P(), P()),
        out_specs=P(("pb", "row")),
        check_vma=False,
    )
```
